256 devices in a mesh: gx: 16 (over y, x), gy: 16 (over z, core).
Axes of the slice: x: 4, y: 4, z: 8, core: 2. Of those that a mesh axis runs over, the one named last changes fastest.
Arguments:
- zonal_wind_field: float32 [32, 128, 2048], P(None, 'gx', 'gy'), may hold values from -6 to 6
- meridional_wind_field: float32 [32, 128, 2048], P(None, 'gx', 'gy'), may hold values from -6 to 6
- vertical_wind_field: float32 [32, 128, 2048], P(None, 'gx', 'gy'), may hold values from -6 to 6
- theta_anomaly_field: float32 [32, 128, 2048], P(None, 'gx', 'gy'), may hold values from -6 to 6
- moisture: float32 [32, 128, 2048], P(None, 'gx', 'gy'), may hold values from -6 to 6
- droplets: float32 [48, 48, 10, 1024], P('gx', 'gy'), may hold values from -6 to 6, as said below
- droplet_cell_index: int32 [48, 48, 1024], P('gx', 'gy'), may hold values from 0 to 32767
- droplet_block_count: int32 [48, 48], P('gx', 'gy'), may hold values from 0 to 1024, as said below
Outputs:
- east_next: float32 [32, 128, 2048], P(None, 'gx', 'gy')
- north_next: float32 [32, 128, 2048], P(None, 'gx', 'gy')
- upward_next: float32 [32, 128, 2048], P(None, 'gx', 'gy')
- heat_next: float32 [32, 128, 2048], P(None, 'gx', 'gy')
- moisture_next: float32 [32, 128, 2048], P(None, 'gx', 'gy')
- droplets_next: float32 [48, 48, 10, 1024], P('gx', 'gy')
The draws below stay inside these ranges and needn't reach their ends.
Inputs may be any that keep to these rules, and one draw needn't show every extreme that they name: `droplets`: rows 0 to 2 of a slot hold position offsets within the cell, in [0, 1); rows 3 to 5 velocities; row 6 the radius, in [0.5, 2]; row 7 the weight, in [0.2, 2]; row 8 the solute mass, in [0.05, 0.5]; row 9 the age, in [0, 2]. Dead slots hold values of the same kinds. `droplet_block_count`: the live droplets of a block fill its first slots. In every draw some device receives 1024 live droplets from each of its nine sources.
All inputs are finite; a program needn't handle non-finite values.
Results may differ from the reference program's by a relative error of at most 0.00075.
Values sent between devices are 32-bit elements; how exact they have to be, the bound alone decides.
No kernel may reach another device: no remote copies, remote signals or barrier semaphores. Data moves between devices by JAX's collectives and lax.ppermute only.
A program may use at most 128 MiB of HBM per device.

```python
import math
import jax
import jax.numpy as jnp
from jax import lax

CX = 8
CY = 128
VERTICAL_LEVELS = 32
CAP = 1024
CELLS_EASTWARD = 128
CELLS_NORTHWARD = 2048
N_GX = 16
N_GY = 16


def draw_vertical_wind_field(key, part):
    key = jax.random.fold_in(key, 11)
    full_shape = (VERTICAL_LEVELS, CX * N_GX, CY * N_GY)
    values = jnp.clip(jax.random.normal(key, full_shape, jnp.float32), -6.0, 6.0)
    return values


def draw_droplets(key, part):
    full_shape = (3 * N_GX, 3 * N_GY, 10, CAP)
    key_unit, key_normal = jax.random.split(key)
    unit_draw = jax.random.uniform(key_unit, full_shape, jnp.float32)
    speeds = jnp.clip(jax.random.normal(key_normal, full_shape, jnp.float32), -6.0, 6.0)
    row_index = lax.broadcasted_iota(jnp.int32, full_shape, 2)
    values = jnp.where(row_index < 3, unit_draw, speeds)
    values = jnp.where(row_index == 6, 0.5 * jnp.exp(unit_draw * math.log(4.0)), values)
    values = jnp.where(row_index == 7, 0.2 * jnp.exp(unit_draw * math.log(10.0)), values)
    values = jnp.where(row_index == 8, 0.05 * jnp.exp(unit_draw * math.log(10.0)), values)
    values = jnp.where(row_index == 9, 2.0 * unit_draw, values)
    return values


def draw_droplet_block_count(key, part):
    grid_shape = (N_GX, 3, N_GY, 3)
    key_level, key_base, key_target = jax.random.split(jax.random.fold_in(key, 7), 3)
    level_draw = jax.random.randint(key_level, (N_GX, 1, N_GY, 1), 2, 6)
    base_draw = jax.random.randint(key_base, grid_shape, CAP // 4, CAP + 1)
    counts = base_draw * level_draw // 5
    target = jax.random.randint(key_target, (2,), 0, 1 << 20)
    target_x = target[0] % N_GX
    target_y = target[1] % N_GY
    dest_x = (lax.broadcasted_iota(jnp.int32, grid_shape, 0) + lax.broadcasted_iota(jnp.int32, grid_shape, 1) - 1) % N_GX
    dest_y = (lax.broadcasted_iota(jnp.int32, grid_shape, 2) + lax.broadcasted_iota(jnp.int32, grid_shape, 3) - 1) % N_GY
    counts = jnp.where((dest_x == target_x) & (dest_y == target_y), CAP, counts)
    return counts.reshape(3 * N_GX, 3 * N_GY)


def with_ends(result, own_key, low, top_value):
    place = [jax.random.randint(jax.random.fold_in(own_key, axis), (), 0, length) for axis, length in enumerate(result.shape)]
    widest = result.shape.index(max(result.shape))
    next_to = place[:widest] + [(place[widest] + 1) % result.shape[widest]] + place[widest + 1:]
    return result.at[tuple(place)].set(low).at[tuple(next_to)].set(top_value)


def block_scale(key, dims, cuts, least, largest):
    factor_of, own = 1.0, jax.random.fold_in(key, 6)
    for dim, blocks in cuts:
        steps = jnp.exp(jax.random.uniform(jax.random.fold_in(own, dim), (blocks,), jnp.float32, least / len(cuts), largest / len(cuts)))
        factor_of = factor_of * jnp.repeat(steps, dims[dim] // blocks).reshape([-1 if axis == dim else 1 for axis in range(len(dims))])
    return factor_of


def normal_values(key, extent, width, reach, cuts=(), kind=jnp.bfloat16):
    result = jax.random.normal(key, extent, jnp.float32) * width
    if len(cuts) > 0:
        result = block_scale(key, extent, cuts, -0.22, 0.18) * result
    return jnp.clip(result, min=-reach, max=reach).astype(kind)


def setup_inputs(seed: int = 0) -> dict:
    streams_of = jax.random.split(jax.random.key(seed), 9)
    zonal_wind_field = normal_values(streams_of[0], (VERTICAL_LEVELS, CELLS_EASTWARD, CELLS_NORTHWARD), 1.0, 6.0, ((1, 16), (2, 16)), jnp.float32)
    meridional_wind_field = normal_values(streams_of[1], (VERTICAL_LEVELS, CELLS_EASTWARD, CELLS_NORTHWARD), 1.0, 6.0, ((1, 16), (2, 16)), jnp.float32)
    vertical_wind_field = draw_vertical_wind_field(jax.random.fold_in(streams_of[8], 71), 0)
    theta_anomaly_field = normal_values(streams_of[3], (VERTICAL_LEVELS, CELLS_EASTWARD, CELLS_NORTHWARD), 1.0, 6.0, ((1, 16), (2, 16)), jnp.float32)
    moisture = normal_values(streams_of[4], (VERTICAL_LEVELS, CELLS_EASTWARD, CELLS_NORTHWARD), 1.0, 6.0, ((1, 16), (2, 16)), jnp.float32)
    droplets = draw_droplets(jax.random.fold_in(streams_of[8], 71), 0)
    droplet_cell_index = with_ends(jax.random.randint(streams_of[6], (3 * N_GX, 3 * N_GY, CAP), 0, VERTICAL_LEVELS * CX * CY), jax.random.fold_in(streams_of[6], 1), 0, (VERTICAL_LEVELS * CX * CY) - 1).astype(jnp.int32)
    droplet_block_count = draw_droplet_block_count(jax.random.fold_in(streams_of[8], 71), 0)
    return dict(zonal_wind_field=zonal_wind_field, meridional_wind_field=meridional_wind_field, vertical_wind_field=vertical_wind_field, theta_anomaly_field=theta_anomaly_field, moisture=moisture, droplets=droplets, droplet_cell_index=droplet_cell_index, droplet_block_count=droplet_block_count)


TIME_STEP = 0.2
RELAX_TIME = 0.2
GROWTH = 0.5
CURVATURE = 0.1
SOLUTE_EFFECT = 0.05
RADIUS_FLOOR = 0.3
SATURATION_RATE = 0.1
MOIST_LOAD = 0.5
HEAT_LOAD = 1.25
CELL_ASPECT = 0.0625
PLUS_TAPS = (-2.0, 15.0, -60.0, 20.0, 30.0, -3.0)
MINUS_TAPS = (3.0, -30.0, -20.0, 60.0, -15.0, 2.0)
HIGHEST = lax.Precision.HIGHEST

def upwind_periodic(quantity, velocity, which_axis):
    plus_side = sum((weight_tap * jnp.roll(quantity, -offset, axis=which_axis) for offset, weight_tap in zip(range(-3, 3), PLUS_TAPS)))
    minus_side = sum((weight_tap * jnp.roll(quantity, -offset, axis=which_axis) for offset, weight_tap in zip(range(-2, 4), MINUS_TAPS)))
    return velocity * jnp.where(velocity >= 0.0, plus_side, minus_side) / 60.0

def upwind_vertical(quantity, velocity, which_axis):
    levels = quantity.shape[which_axis]
    widths = [(0, 0)] * quantity.ndim
    widths[which_axis] = (3, 3)
    padded = jnp.pad(quantity, widths, mode='edge')
    plus_side = sum((weight_tap * lax.slice_in_dim(padded, 3 + offset, 3 + offset + levels, axis=which_axis) for offset, weight_tap in zip(range(-3, 3), PLUS_TAPS)))
    minus_side = sum((weight_tap * lax.slice_in_dim(padded, 3 + offset, 3 + offset + levels, axis=which_axis) for offset, weight_tap in zip(range(-2, 4), MINUS_TAPS)))
    return velocity * jnp.where(velocity >= 0.0, plus_side, minus_side) / 60.0

def cosine_table(levels):
    mode_index = lax.broadcasted_iota(jnp.int32, (levels, levels), 0)
    level_index = lax.broadcasted_iota(jnp.int32, (levels, levels), 1)
    phases = (mode_index * (2 * level_index + 1) % (4 * levels)).astype(jnp.float32) * (math.pi / (2 * levels))
    factor = jnp.where(mode_index == 0, math.sqrt(1.0 / levels), math.sqrt(2.0 / levels))
    return factor * jnp.cos(phases)

def hartley(values, which_axis):
    spectrum = jnp.fft.fft(values, axis=which_axis)
    return (spectrum.real - spectrum.imag) / math.sqrt(values.shape[which_axis])

def eigen_value(wave_index, period):
    return 2.0 - 2.0 * jnp.cos((wave_index % period).astype(jnp.float32) * (2.0 * math.pi / period))

def arrivals(values):
    grid_view = values.reshape((N_GX, 3, N_GY, 3) + values.shape[2:])
    row_blocks = []
    for row_slot in range(3):
        col_blocks = []
        for col_slot in range(3):
            source = grid_view[:, 2 - row_slot, :, 2 - col_slot]
            col_blocks.append(jnp.roll(source, (1 - row_slot, 1 - col_slot), axis=(0, 1)))
        row_blocks.append(jnp.stack(col_blocks, axis=2))
    return jnp.stack(row_blocks, axis=1).reshape(values.shape)

def grow_droplets(attributes, air_east, air_north, air_upward, air_heat, air_moist, live_slots):
    radius = attributes[..., 6, :]
    radius_cubed = radius * radius * radius
    keeping = jnp.exp(-TIME_STEP / (RELAX_TIME * radius * radius))
    east_speed = air_east + (attributes[..., 3, :] - air_east) * keeping
    north_speed = air_north + (attributes[..., 4, :] - air_north) * keeping
    rise_speed = air_upward + (attributes[..., 5, :] - air_upward) * keeping
    saturation = air_moist * jnp.exp(-SATURATION_RATE * air_heat) - 1.0
    squared = radius * radius + GROWTH * (saturation - CURVATURE / radius + SOLUTE_EFFECT * attributes[..., 8, :] / radius_cubed)
    new_radius = jnp.sqrt(jnp.maximum(squared, RADIUS_FLOOR * RADIUS_FLOOR))
    water_gain = live_slots * attributes[..., 7, :] * (new_radius * new_radius * new_radius - radius_cubed)
    rows_out = [attributes[..., 0, :] + TIME_STEP * east_speed, attributes[..., 1, :] + TIME_STEP * north_speed, attributes[..., 2, :] + TIME_STEP * rise_speed, east_speed, north_speed, rise_speed, new_radius, attributes[..., 7, :], attributes[..., 8, :], attributes[..., 9, :] + TIME_STEP]
    moved_drops = jnp.stack(rows_out, axis=-2) * live_slots[..., None, :]
    return (moved_drops, water_gain)

def reference(zonal_wind_field, meridional_wind_field, vertical_wind_field, theta_anomaly_field, moisture, droplets, droplet_cell_index, droplet_block_count):
    prognostic_fields = (zonal_wind_field, meridional_wind_field, vertical_wind_field, theta_anomaly_field, moisture)
    starred = []
    for quantity in prognostic_fields:
        tendency = upwind_periodic(quantity, zonal_wind_field, 1) + upwind_periodic(quantity, meridional_wind_field, 2) + upwind_vertical(quantity, vertical_wind_field, 0)
        starred.append(quantity - TIME_STEP * tendency)
    east_star, north_star, upward_star, heat_star, moist_star = starred
    levels, total_x, total_y = zonal_wind_field.shape
    level_index = lax.broadcasted_iota(jnp.int32, upward_star.shape, 0)
    upward_star = jnp.where(level_index == levels - 1, 0.0, upward_star)
    upward_below = jnp.concatenate([jnp.zeros_like(upward_star[:1]), upward_star[:-1]], axis=0)
    diverge = east_star - jnp.roll(east_star, 1, axis=1) + (north_star - jnp.roll(north_star, 1, axis=2)) + (upward_star - upward_below)
    ztable = cosine_table(levels)
    source_hat = jnp.einsum('mk,kxy->mxy', ztable, diverge, precision=HIGHEST)
    source_hat = hartley(hartley(source_hat, 1), 2)
    mode_index = lax.broadcasted_iota(jnp.int32, (levels, 1, 1), 0)
    wave_x = lax.broadcasted_iota(jnp.int32, (1, total_x, 1), 1)
    wave_y = lax.broadcasted_iota(jnp.int32, (1, 1, total_y), 2)
    eigen_sum = (eigen_value(mode_index, 2 * levels) + eigen_value(wave_x, total_x)) * CELL_ASPECT + eigen_value(wave_y, total_y)
    zero_mode = (mode_index == 0) & (wave_x == 0) & (wave_y == 0)
    pressure_hat = jnp.where(zero_mode, 0.0, -source_hat / jnp.where(zero_mode, 1.0, eigen_sum))
    pressure = hartley(hartley(pressure_hat, 2), 1)
    pressure = jnp.einsum('mk,mxy->kxy', ztable, pressure, precision=HIGHEST)
    east_grad = (jnp.roll(pressure, -1, axis=1) - pressure) * CELL_ASPECT
    north_grad = jnp.roll(pressure, -1, axis=2) - pressure
    upward_grad = jnp.concatenate([pressure[1:] - pressure[:-1], jnp.zeros_like(pressure[:1])], axis=0) * CELL_ASPECT
    east_next = east_star - east_grad
    north_next = north_star - north_grad
    upward_next = upward_star - upward_grad
    moved_in = arrivals(droplets)
    cells_in = arrivals(droplet_cell_index)
    counts_in = arrivals(droplet_block_count)
    block_shape = cells_in.shape
    device_x = lax.broadcasted_iota(jnp.int32, block_shape, 0) // 3
    device_y = lax.broadcasted_iota(jnp.int32, block_shape, 1) // 3
    slot_index = lax.broadcasted_iota(jnp.int32, block_shape, 2)
    live_slots = (slot_index < counts_in[:, :, None]).astype(jnp.float32)
    level_of = cells_in // (CX * CY)
    column_x = cells_in // CY % CX
    column_y = cells_in % CY
    flat_index = (level_of * CELLS_EASTWARD + device_x * CX + column_x) * CELLS_NORTHWARD + device_y * CY + column_y
    air_values = [quantity.reshape(-1)[flat_index] for quantity in (east_next, north_next, upward_next, heat_star, moist_star)]
    moved_drops, water_gain = grow_droplets(moved_in, air_values[0], air_values[1], air_values[2], air_values[3], air_values[4], live_slots)
    condensed = jnp.zeros((levels * total_x * total_y,), jnp.float32).at[flat_index.reshape(-1)].add(water_gain.reshape(-1))
    condensed = condensed.reshape(levels, total_x, total_y)
    heat_next = heat_star + HEAT_LOAD * condensed
    moisture_next = moist_star - MOIST_LOAD * condensed
    return (east_next, north_next, upward_next, heat_next, moisture_next, moved_drops)
```

```python
import math

import jax
import jax.numpy as jnp
import numpy as np
from jax import lax
from jax.experimental import pallas as pl
from jax.experimental.pallas import tpu as pltpu
from jax.sharding import PartitionSpec as P

DT = 0.2
RELAX_TIME = 0.2
GROWTH = 0.5
CURVATURE = 0.1
SOLUTE_EFFECT = 0.05
RADIUS_FLOOR = 0.3
SATURATION_RATE = 0.1
MOIST_LOAD = 0.5
HEAT_LOAD = 1.25
ASPECT = 0.0625
HIGHEST = lax.Precision.HIGHEST

NZ = 32
NX = 8
NY = 128
GX = 16
GY = 16
TX = NX * GX
TY = NY * GY
CAP = 1024
ROWS = NZ * NX
SLOT = 12
BLK = 2 * SLOT
F32 = jnp.float32
BF16 = jnp.bfloat16


def make_tables():
    m = np.arange(NZ)
    ztab = np.cos(np.pi * m[:, None] * (2 * m[None, :] + 1) / (2 * NZ)) * np.where(
        m[:, None] == 0, math.sqrt(1.0 / NZ), math.sqrt(2.0 / NZ)
    )
    zdiff = np.zeros((NZ, NZ))
    zdiff[:-1] = (ztab.T[1:] - ztab.T[:-1]) * ASPECT
    zback = np.concatenate([ztab.T, zdiff], axis=0)
    p = np.arange(TX)

    def cas(a):
        return np.cos(a) + np.sin(a)

    w = 2 * np.pi / TX
    har = cas(w * (p[:, None] * p[None, :] % TX)) / math.sqrt(TX)
    wmain = np.zeros((2, TX, GX, 2, SLOT))
    for X in range(GX):
        for t in range(NX + 1):
            for b in range(2):
                wmain[b, :, X, b, t] = har[:, (NX * X + t) % TX]
    wmain = wmain.reshape(2 * TX, GX * BLK)
    X = np.arange(GX)
    t12 = np.concatenate(
        [cas(w * p[:, None] * NX * X[None, :]), cas(-w * p[:, None] * NX * X[None, :])], axis=0
    ) / math.sqrt(TX)
    lane = np.arange(NY)
    cosx = np.where(lane[None, :] < NX, np.cos(w * p[:, None] * lane[None, :]), 0.0)
    sinx = np.where(lane[None, :] < NX, np.sin(w * p[:, None] * lane[None, :]), 0.0)
    cs = np.concatenate([cosx, sinx], axis=0)
    lam = (
        (2 - 2 * np.cos(np.pi * m[:, None] / NZ)) + (2 - 2 * np.cos(w * p[None, :]))
    ) * ASPECT
    zero = lam <= 0
    lam = np.where(zero, 0.5, lam)
    lnr = -2.0 * np.arcsinh(np.sqrt(lam) / 2.0)
    coef = np.where(zero, 0.0, -1.0 / (2.0 * np.sinh(-lnr)))
    lnr = lnr.reshape(2, GX, TX).transpose(1, 0, 2).reshape(GX, 2 * TX)
    coef = coef.reshape(2, GX, TX).transpose(1, 0, 2).reshape(GX, 2 * TX)
    rpow = np.exp(lnr[:, :, None] * lane)
    rrev = np.exp(lnr[:, :, None] * (NY - lane))
    misc = np.zeros((GX, 2 * TX, NY))
    for k in range(8):
        misc[:, :, k] = np.exp(lnr * (1 << k))
    misc[:, :, 8] = coef
    rowtab = np.zeros((GX, 8, 2 * TX))
    rowtab[:, 0] = NY * lnr
    rowtab[:, 1] = 1.0 / (1.0 - np.exp(lnr * TY))
    absd = np.abs(lane[:, None] - lane[None, :])

    def f(a):
        return jnp.asarray(np.asarray(a, np.float32))

    return dict(
        ztab=f(ztab),
        zback=f(zback),
        wmain=f(wmain),
        wback=f(wmain.T),
        t12=f(t12),
        t12t=f(t12.T),
        cs=f(cs),
        rpow=f(rpow),
        rrev=f(rrev),
        misc=f(misc),
        rowtab=f(rowtab),
        absd=f(absd),
    )


def iota(shape, dim):
    return lax.broadcasted_iota(jnp.int32, shape, dim)


def dot(a, b):
    return jnp.dot(a, b, precision=HIGHEST, preferred_element_type=F32)


def row_of(ref, x):
    return ref[pl.ds(x, NZ, stride=NX), :]


def pair_of(f0, lo, hi):
    d1, d2, d3 = (h - l for l, h in zip(lo, hi))
    s1, s2, s3 = (h + l for l, h in zip(lo, hi))
    return (45.0 * d1 - 9.0 * d2 + d3, 20.0 * f0 - 15.0 * s1 + 6.0 * s2 - s3)


def star_row(x, rows, ylo, yhi, slot, velocity, zs, lane):
    f0 = rows[x + 3]
    zs[8 : 8 + NZ, :] = f0
    zs[0:8, :] = jnp.broadcast_to(f0[0:1], (8, NY))
    zs[8 + NZ : 16 + NZ, :] = jnp.broadcast_to(f0[NZ - 1 : NZ], (8, NY))
    au, bu, av, bv, aw, bw = velocity
    a, b = pair_of(
        f0, [rows[x + 3 - k] for k in (1, 2, 3)], [rows[x + 3 + k] for k in (1, 2, 3)]
    )
    total = au * a + bu * b
    where_lo = 16 * x + 3 * slot
    halo = jnp.where(
        lane >= 64,
        pltpu.roll(ylo, (125 - where_lo) % NY, 1),
        pltpu.roll(yhi, (NY - where_lo) % NY, 1),
    )
    lo = [pltpu.roll(jnp.where(lane >= NY - k, halo, f0), k, 1) for k in (1, 2, 3)]
    hi = [pltpu.roll(jnp.where(lane < k, halo, f0), NY - k, 1) for k in (1, 2, 3)]
    a, b = pair_of(f0, lo, hi)
    total = total + (av * a + bv * b)
    a, b = pair_of(
        f0,
        [zs[8 - k : 8 - k + NZ, :] for k in (1, 2, 3)],
        [zs[8 + k : 8 + k + NZ, :] for k in (1, 2, 3)],
    )
    return f0 - (total + (aw * a + bw * b))


def velocity_rows(u, v, w, x):
    out = []
    for ref in (u, v, w):
        a = row_of(ref, x) * (DT / 60.0)
        out += [a, jnp.abs(a)]
    return out


def yhalo_of(msg):
    return jnp.concatenate([msg[40:48, g * NY : (g + 1) * NY] for g in range(4)], axis=0)


def pack_blocks(out, blocks):
    for n, (drops, cells, count) in enumerate(blocks):
        out[n * SLOT : n * SLOT + 10, :] = drops
        out[n * SLOT + 10 : n * SLOT + 11, :] = cells
        out[n * SLOT + 11 : n * SLOT + 12, :] = count
    out[36:40, :] = jnp.zeros((4, CAP), F32)


def own_block(drops, cells, counts, n):
    return (
        drops[n],
        cells[n : n + 1, :].astype(F32),
        jnp.full((1, CAP), counts[n], jnp.int32).astype(F32),
    )


def pack_kernel(u, v, w, h, q, drops, cells, counts, xlo, xhi, up, down):
    for f, ref in enumerate((u, v, w)):
        for i in range(3):
            n = f * 3 + i
            xlo[n * NZ : (n + 1) * NZ, :] = row_of(ref, 5 + i)
            xhi[n * NZ : (n + 1) * NZ, :] = row_of(ref, i)
    lane = iota((NZ, NY), 1)
    tlo = jnp.zeros((NZ, NY), F32)
    thi = jnp.zeros((NZ, NY), F32)
    for x in range(NX):
        for f, ref in enumerate((u, v, w, h, q)):
            at = 16 * x + 3 * f
            row = row_of(ref, x)
            mask = (lane >= at) & (lane < at + 3)
            tlo = jnp.where(mask, pltpu.roll(row, (at - 125) % NY, 1), tlo)
            thi = jnp.where(mask, pltpu.roll(row, at, 1), thi)
    for out, tile, s in ((up, tlo, 2), (down, thi, 0)):
        pack_blocks(out, [own_block(drops, cells, counts, r * 3 + s) for r in range(3)])
        for g in range(4):
            out[40:48, g * NY : (g + 1) * NY] = tile[g * 8 : (g + 1) * 8]
        out[40:48, 4 * NY :] = jnp.zeros((8, 4 * NY), F32)


def block_of(msg, n):
    return (
        msg[n * SLOT : n * SLOT + 10, :],
        msg[n * SLOT + 10 : n * SLOT + 11, :],
        msg[n * SLOT + 11 : n * SLOT + 12, :],
    )


def relay_kernel(h, q, drops, cells, counts, mlo, mhi, up, down):
    for out, r, x0 in ((up, 2, 5), (down, 0, 0)):
        pack_blocks(
            out,
            [block_of(mlo, r), own_block(drops, cells, counts, r * 3 + 1), block_of(mhi, r)],
        )
        for f, ref in enumerate((h, q)):
            for i in range(3):
                row = row_of(ref, x0 + i)
                for g in range(4):
                    n = (f * 3 + i) * 4 + g
                    a, c = 40 + 8 * (n // 8), NY * (n % 8)
                    out[a : a + 8, c : c + NY] = row[g * 8 : (g + 1) * 8]


def wind_kernel(u, v, w, xlo, xhi, mlo, mhi, ztab, stars, send, zs):
    lane = iota((NZ, NY), 1)
    level = iota((NZ, NY), 0)
    ylo = yhalo_of(mlo)
    yhi = yhalo_of(mhi)
    vel = [velocity_rows(u, v, w, x) for x in range(NX)]
    for f, ref in enumerate((u, v, w)):
        rows = [xlo[(f * 3 + i) * NZ : (f * 3 + i + 1) * NZ, :] for i in range(3)]
        rows += [row_of(ref, x) for x in range(NX)]
        rows += [xhi[(f * 3 + i) * NZ : (f * 3 + i + 1) * NZ, :] for i in range(3)]
        for x in range(NX):
            star = star_row(x, rows, ylo, yhi, f, vel[x], zs.at[f * NX + x], lane)
            if f == 2:
                star = jnp.where(level == NZ - 1, 0.0, star)
            at = (f * NX + x) * NZ
            stars[at : at + NZ, :] = star
    tiles = []
    ext = jnp.zeros((NZ, NY), F32)
    for x in range(NX):
        east = stars[x * NZ : (x + 1) * NZ, :]
        north = stars[(NX + x) * NZ : (NX + x + 1) * NZ, :]
        rise = stars[(2 * NX + x) * NZ : (2 * NX + x + 1) * NZ, :]
        d = east + north + rise
        if x > 0:
            d = d - stars[(x - 1) * NZ : x * NZ, :]
        d = d - jnp.where(lane == 0, 0.0, pltpu.roll(north, 1, 1))
        d = d - jnp.where(level == 0, 0.0, pltpu.roll(rise, 1, 0))
        tiles.append(d)
        ext = jnp.where(lane == x, -pltpu.roll(north, (x + 1) % NY, 1), ext)
    tiles.append(-stars[(NX - 1) * NZ : NX * NZ, :])
    tiles.append(ext)
    hat = dot(ztab[...], jnp.concatenate(tiles, axis=1))
    zeros = jnp.zeros((GX, NY), F32)
    for b in range(2):
        for t in range(SLOT):
            if t < NX + 2:
                val = hat[b * GX : (b + 1) * GX, t * NY : (t + 1) * NY]
            else:
                val = zeros
            send[pl.ds(b * SLOT + t, GX, stride=BLK), :] = val


def scan_kernel(sx, recv, wmain, t12, cs, rrev, misc, absd, msg, keep, cols, kink):
    lane = iota((2 * TX, NY), 1)
    d = dot(wmain[...], recv[...])
    ends = []
    for b in range(2):
        e16 = recv[pl.ds(b * SLOT + NX + 1, GX, stride=BLK), :]
        prod = dot(t12[...], e16) * cs[...]
        ends.append(jnp.sum(prod[:TX] + prod[TX:], axis=1, keepdims=True))
    e = jnp.concatenate(ends, axis=0)
    fwd = d
    bwd = d
    for k in range(7):
        s = 1 << k
        a = jnp.broadcast_to(misc[0, :, k : k + 1], (2 * TX, NY))
        fwd = fwd + jnp.where(lane >= s, a * pltpu.roll(fwd, s, 1), 0.0)
        bwd = bwd + jnp.where(lane < NY - s, a * pltpu.roll(bwd, NY - s, 1), 0.0)
    r1 = misc[0, :, 0:1]
    r128 = misc[0, :, 7:8]
    out_right = r1 * fwd[:, NY - 1 : NY] + e
    out_left = bwd[:, 0:1] + r128 * e
    keep[...] = fwd + bwd - d + rrev[0] * e
    table = jnp.where(lane == 0, out_right, jnp.where(lane == 1, out_left, 0.0))
    d8 = d[0:8]
    e8 = e[0:8]
    lane8 = iota((8, NY), 1)
    lanef = lane8.astype(F32)
    s0 = jnp.sum(d8, axis=1, keepdims=True) + e8
    s1 = jnp.sum(d8 * lanef, axis=1, keepdims=True) + float(NY) * e8
    top = jnp.where(lane8 == 2, s0, jnp.where(lane8 == 3, s1, table[0:8]))
    table = jnp.concatenate([top, table[8:]], axis=0)
    cols[...] = table
    turned = table.T[0:8]
    for y in range(GY):
        msg[y * 8 : (y + 1) * 8, :] = turned
    kink[...] = dot(d8, absd[...]) + e8 * (float(NY) - lanef)


def solve_kernel(sx, got, keep, cols, kink, wback, t12t, cs, rpow, rrev, misc, rowtab, send):
    here = sx[1]
    first = (sx[0] == 0).astype(F32)
    who = iota((GY, 2 * TX), 0)
    all_right = jnp.concatenate([got[y * 8 : y * 8 + 1, :] for y in range(GY)], axis=0)
    all_left = jnp.concatenate([got[y * 8 + 1 : y * 8 + 2, :] for y in range(GY)], axis=0)
    s0 = jnp.concatenate([got[y * 8 + 2 : y * 8 + 3, 0:1] for y in range(GY)], axis=0)
    s1 = jnp.concatenate([got[y * 8 + 3 : y * 8 + 4, 0:1] for y in range(GY)], axis=0)
    lnr = rowtab[0, 0:1, :]
    inv = rowtab[0, 1:2, :]
    after = ((here - who - 1) & (GY - 1)).astype(F32)
    before = ((who - here - 1) & (GY - 1)).astype(F32)
    in_left = jnp.sum(jnp.exp(after * lnr) * all_right, axis=0, keepdims=True) * inv
    in_right = jnp.sum(jnp.exp(before * lnr) * all_left, axis=0, keepdims=True) * inv
    row = iota((8, 2 * TX), 0)
    turned = jnp.where(row == 0, in_left, jnp.where(row == 1, in_right, 0.0)).T
    in_left = turned[:, 0:1]
    in_right = turned[:, 1:2]
    coef = misc[0, :, 8:9]
    pres = coef * (keep[...] + rpow[0] * in_left + rrev[0] * in_right)
    edge = coef * (cols[:, 0:1] + misc[0, :, 7:8] * in_left + in_right)
    who1 = iota((GY, 1), 0)
    far = (NY * ((here - who1) & (GY - 1))).astype(F32)
    mine = who1 == here
    sum0 = jnp.sum(s0, axis=0, keepdims=True)
    own0 = jnp.sum(jnp.where(mine, s0, 0.0), axis=0, keepdims=True)
    own1 = jnp.sum(jnp.where(mine, s1, 0.0), axis=0, keepdims=True)
    lin = 0.5 * (sum0 - own0) + jnp.sum(s1 - far * s0, axis=0, keepdims=True) * (1.0 / TY)
    quad = sum0 * (0.5 / TY)
    lanef = iota((8, NY), 1).astype(F32)
    top = 0.5 * kink[...] + lanef * (lin - lanef * quad)
    edge0 = 0.5 * (float(NY) * own0 - own1) + float(NY) * (lin - float(NY) * quad)
    row8 = iota((8, NY), 0)
    top = pres[0:8] + jnp.where(row8 == 0, first * top, 0.0)
    pres = jnp.concatenate([top, pres[8:]], axis=0)
    row1 = iota((2 * TX, 1), 0)
    edge = edge + jnp.where(row1 == 0, first * edge0, 0.0)
    send[...] = dot(wback[...], pres)
    for b in range(2):
        eb = edge[b * TX : (b + 1) * TX]
        spread = jnp.concatenate([cs[0:TX, :] * eb, cs[TX:, :] * eb], axis=0)
        send[pl.ds(b * SLOT + NX + 1, GX, stride=BLK), :] = dot(t12t[...], spread)


def store_table(lhs, n, table):
    turned = table.T
    hi = turned.astype(BF16)
    lhs[n * NY : (n + 1) * NY, :] = hi
    lhs[(n + 1) * NY : (n + 2) * NY, :] = (turned - hi.astype(F32)).astype(BF16)


def masks_of(cells):
    width = cells.shape[1]
    rowid = ((cells >> 7) & (NX - 1)) * NZ + (cells >> 10)
    hot = jnp.where(iota((ROWS, width), 0) == rowid, 1.0, 0.0).astype(BF16)
    pick = iota((NY, width), 0) == (cells & (NY - 1))
    return hot, pick


def gather_one(lhs, n, hot, pick):
    hi = jnp.dot(lhs[n * NY : (n + 1) * NY, :], hot, preferred_element_type=F32)
    lo = jnp.dot(lhs[(n + 1) * NY : (n + 2) * NY, :], hot, preferred_element_type=F32)
    return jnp.sum(jnp.where(pick, hi + lo, 0.0), axis=0, keepdims=True)


CHUNK = 512


def drop_kernel(
    u, v, w, h, q, mlo, mhi, clo, chi, drops, cells, counts,
    heat_next, moist_next, cell_out, state, zs, stars, lhs, acc, air,
):
    lane = iota((NZ, NY), 1)
    ylo = yhalo_of(mlo)
    yhi = yhalo_of(mhi)
    vel = [velocity_rows(u, v, w, x) for x in range(NX)]

    def side(msg, n):
        parts = []
        for g in range(4):
            k = n * 4 + g
            a, c = 40 + 8 * (k // 8), NY * (k % 8)
            parts.append(msg[a : a + 8, c : c + NY])
        return jnp.concatenate(parts, axis=0)

    for f, ref in enumerate((h, q)):
        rows = [side(clo, f * 3 + i) for i in range(3)]
        rows += [row_of(ref, x) for x in range(NX)]
        rows += [side(chi, f * 3 + i) for i in range(3)]
        for x in range(NX):
            star = star_row(x, rows, ylo, yhi, 3 + f, vel[x], zs.at[f * NX + x], lane)
            at = (f * NX + x) * NZ
            stars[at : at + NZ, :] = star
        store_table(lhs, 2 * f, stars[f * ROWS : (f + 1) * ROWS, :])
    for r in range(3):
        for s in range(3):
            n = r * 3 + s
            if r == 0:
                block = block_of(clo, s)
            elif r == 2:
                block = block_of(chi, s)
            elif s == 0:
                block = block_of(mlo, 1)
            elif s == 2:
                block = block_of(mhi, 1)
            else:
                block = own_block(drops, cells, counts, 4)
            values, cell, count = block
            for a in range(10):
                state[a, n : n + 1, :] = values[a : a + 1]
            cell_out[n : n + 1, :] = cell.astype(jnp.int32)
            slot = iota((1, CAP), 1).astype(F32)
            state[10, n : n + 1, :] = jnp.where(slot < count, 1.0, 0.0)

    def gather_block(n, carry):
        for c in range(CAP // CHUNK):
            at = c * CHUNK
            hot, pick = masks_of(cell_out[pl.ds(n, 1), at : at + CHUNK])
            for f in range(2):
                air[f, pl.ds(n, 1), at : at + CHUNK] = gather_one(lhs, 2 * f, hot, pick)
        return carry

    lax.fori_loop(0, 9, gather_block, 0)
    live = state[10]
    radius = state[6]
    cubed = radius * radius * radius
    keeping = jnp.exp(-DT / (RELAX_TIME * radius * radius))
    saturation = air[1] * jnp.exp(-SATURATION_RATE * air[0]) - 1.0
    squared = radius * radius + GROWTH * (
        saturation - CURVATURE / radius + SOLUTE_EFFECT * state[8] / cubed
    )
    new_radius = jnp.sqrt(jnp.maximum(squared, RADIUS_FLOOR * RADIUS_FLOOR))
    gain = live * state[7] * (new_radius * new_radius * new_radius - cubed)
    air[0] = gain
    state[6] = new_radius * live
    state[7] = state[7] * live
    state[8] = state[8] * live
    state[9] = (state[9] + DT) * live
    for a in range(3):
        state[a] = state[a] * live
        state[3 + a] = state[3 + a] * (keeping * live)
    state[10] = (1.0 - keeping) * live
    acc[...] = jnp.zeros_like(acc)

    def scatter_block(n, carry):
        for c in range(CAP // CHUNK):
            at = c * CHUNK
            hot, pick = masks_of(cell_out[pl.ds(n, 1), at : at + CHUNK])
            g = air[0, pl.ds(n, 1), at : at + CHUNK]
            hi = g.astype(BF16).astype(F32)
            lo = g - hi
            z = jnp.concatenate(
                [
                    jnp.where(pick, hi, 0.0).astype(BF16),
                    jnp.where(pick, lo, 0.0).astype(BF16),
                ],
                axis=0,
            )
            acc[...] += lax.dot_general(
                hot, z, (((1,), (1,)), ((), ())), preferred_element_type=F32
            )
        return carry

    lax.fori_loop(0, 9, scatter_block, 0)
    for x in range(NX):
        a = x * NZ
        condensed = acc[a : a + NZ, 0:NY] + acc[a : a + NZ, NY:]
        heat_next[pl.ds(x, NZ, stride=NX), :] = stars[a : a + NZ, :] + HEAT_LOAD * condensed
        moist_next[pl.ds(x, NZ, stride=NX), :] = (
            stars[ROWS + a : ROWS + a + NZ, :] - MOIST_LOAD * condensed
        )


def final_kernel(
    recv, stars, zback, cell, state, east_next, north_next, up_next, drops_out, lhs, next_rows, air
):
    lane = iota((NZ, NY), 1)
    tiles = []
    for t in range(NX + 2):
        tiles.append(
            jnp.concatenate(
                [recv[pl.ds(b * SLOT + t, GX, stride=BLK), :] for b in range(2)], axis=0
            )
        )
    both = dot(zback[...], jnp.concatenate(tiles, axis=1))
    pres = [both[:NZ, t * NY : (t + 1) * NY] for t in range(NX + 2)]
    edge = pres[NX + 1]
    for x in range(NX):
        east = stars[x * NZ : (x + 1) * NZ, :] - (pres[x + 1] - pres[x]) * ASPECT
        ahead = pltpu.roll(
            jnp.where(lane == 0, pltpu.roll(edge, (NY - x) % NY, 1), pres[x]), NY - 1, 1
        )
        north = stars[(NX + x) * NZ : (NX + x + 1) * NZ, :] - (ahead - pres[x])
        rise = (
            stars[(2 * NX + x) * NZ : (2 * NX + x + 1) * NZ, :]
            - both[NZ:, x * NY : (x + 1) * NY]
        )
        for f, (val, ref) in enumerate(
            ((east, east_next), (north, north_next), (rise, up_next))
        ):
            ref[pl.ds(x, NZ, stride=NX), :] = val
            next_rows[f, x * NZ : (x + 1) * NZ, :] = val
    for f in range(3):
        store_table(lhs, 2 * f, next_rows[f])

    def gather_block(n, carry):
        for c in range(CAP // CHUNK):
            at = c * CHUNK
            hot, pick = masks_of(cell[pl.ds(n, 1), at : at + CHUNK])
            for f in range(3):
                air[f, pl.ds(n, 1), at : at + CHUNK] = gather_one(lhs, 2 * f, hot, pick)
        return carry

    lax.fori_loop(0, 9, gather_block, 0)
    mix = state[10]
    for a in range(3):
        speed = air[a] * mix + state[3 + a]
        offset = state[a] + DT * speed
        for n in range(9):
            drops_out[n, 3 + a : 4 + a, :] = speed[n : n + 1]
            drops_out[n, a : a + 1, :] = offset[n : n + 1]
    for n in range(9):
        for a in range(6, 10):
            drops_out[n, a : a + 1, :] = state[a, n : n + 1, :]


VM = pl.BlockSpec(memory_space=pltpu.VMEM)
SM = pl.BlockSpec(memory_space=pltpu.SMEM)


def sds(*shape, dtype=F32):
    return jax.ShapeDtypeStruct(shape, dtype)


def params():
    return pltpu.CompilerParams(vmem_limit_bytes=48 * 1024 * 1024)


def cost(us):
    return pl.CostEstimate(flops=int(us * 5e8), bytes_accessed=int(us * 2e6), transcendentals=0)


def whole(shape):
    zeros = (0,) * len(shape)
    return pl.BlockSpec(shape, lambda i, s: zeros)


def chosen(shape):
    zeros = (0,) * (len(shape) - 1)
    return pl.BlockSpec(shape, lambda i, s: (s[0],) + zeros)


def ring(axis, shift):
    count = lax.axis_size(axis)
    return [(i, (i + shift) % count) for i in range(count)]


def per_device(u, v, w, h, q, droplets, cell_index, block_count):
    tab = make_tables()
    u, v, w, h, q = (a.reshape(ROWS, NY) for a in (u, v, w, h, q))
    drops = droplets.reshape(9, 10, CAP)
    cells = cell_index.reshape(9, CAP)
    counts = block_count.reshape(9)
    xlo, xhi, up, down = pl.pallas_call(
        pack_kernel,
        out_shape=(sds(9 * NZ, NY), sds(9 * NZ, NY), sds(48, CAP), sds(48, CAP)),
        in_specs=[VM] * 7 + [SM],
        out_specs=(VM,) * 4,
        compiler_params=params(),
        cost_estimate=cost(1.5),
        name="pack",
    )(u, v, w, h, q, drops, cells, counts)
    xlo = lax.ppermute(xlo, "gx", ring("gx", 1))
    xhi = lax.ppermute(xhi, "gx", ring("gx", -1))
    mlo = lax.ppermute(up, "gy", ring("gy", 1))
    mhi = lax.ppermute(down, "gy", ring("gy", -1))
    cup, cdown = pl.pallas_call(
        relay_kernel,
        out_shape=(sds(64, CAP), sds(64, CAP)),
        in_specs=[VM] * 4 + [SM] + [VM] * 2,
        out_specs=(VM, VM),
        compiler_params=params(),
        cost_estimate=cost(1.0),
        name="relay",
    )(h, q, drops, cells, counts, mlo, mhi)
    clo = lax.ppermute(cup, "gx", ring("gx", 1))
    chi = lax.ppermute(cdown, "gx", ring("gx", -1))
    stars, send = pl.pallas_call(
        wind_kernel,
        out_shape=(sds(3 * ROWS, NY), sds(GX * BLK, NY)),
        in_specs=[VM] * 8,
        out_specs=(VM, VM),
        scratch_shapes=[pltpu.VMEM((3 * NX, NZ + 16, NY), F32)],
        compiler_params=params(),
        cost_estimate=cost(3.0),
        name="winds",
    )(u, v, w, xlo, xhi, mlo, mhi, tab["ztab"])
    recv = lax.all_to_all(send.reshape(GX, BLK, NY), "gx", 0, 0, tiled=True)
    heat_next, moist_next, cell_in, state = pl.pallas_call(
        drop_kernel,
        out_shape=(
            sds(ROWS, NY), sds(ROWS, NY), sds(9, CAP, dtype=jnp.int32), sds(11, 9, CAP),
        ),
        in_specs=[VM] * 11 + [SM],
        out_specs=(VM,) * 4,
        scratch_shapes=[
            pltpu.VMEM((2 * NX, NZ + 16, NY), F32),
            pltpu.VMEM((2 * ROWS, NY), F32),
            pltpu.VMEM((4 * NY, ROWS), BF16),
            pltpu.VMEM((ROWS, 2 * NY), F32),
            pltpu.VMEM((2, 9, CAP), F32),
        ],
        compiler_params=params(),
        cost_estimate=cost(10.0),
        name="growth",
    )(u, v, w, h, q, mlo, mhi, clo, chi, drops, cells, counts)
    place = jnp.stack([lax.axis_index("gx"), lax.axis_index("gy")]).astype(jnp.int32)
    msg, keep, cols, kink = pl.pallas_call(
        scan_kernel,
        out_shape=(sds(8 * GY, 2 * TX), sds(2 * TX, NY), sds(2 * TX, NY), sds(8, NY)),
        grid_spec=pltpu.PrefetchScalarGridSpec(
            num_scalar_prefetch=1,
            grid=(1,),
            in_specs=[
                whole((GX * BLK, NY)),
                whole((2 * TX, GX * BLK)),
                whole((2 * TX, GX)),
                whole((2 * TX, NY)),
                chosen((1, 2 * TX, NY)),
                chosen((1, 2 * TX, NY)),
                whole((NY, NY)),
            ],
            out_specs=[
                whole((8 * GY, 2 * TX)), whole((2 * TX, NY)), whole((2 * TX, NY)), whole((8, NY)),
            ],
        ),
        compiler_params=params(),
        cost_estimate=cost(2.0),
        name="scan",
    )(
        place, recv.reshape(GX * BLK, NY), tab["wmain"], tab["t12"], tab["cs"],
        tab["rrev"], tab["misc"], tab["absd"],
    )
    got = lax.all_to_all(msg.reshape(GY, 8, 2 * TX), "gy", 0, 0, tiled=True)
    send = pl.pallas_call(
        solve_kernel,
        out_shape=sds(GX * BLK, NY),
        grid_spec=pltpu.PrefetchScalarGridSpec(
            num_scalar_prefetch=1,
            grid=(1,),
            in_specs=[
                whole((8 * GY, 2 * TX)),
                whole((2 * TX, NY)),
                whole((2 * TX, NY)),
                whole((8, NY)),
                whole((GX * BLK, 2 * TX)),
                whole((GX, 2 * TX)),
                whole((2 * TX, NY)),
                chosen((1, 2 * TX, NY)),
                chosen((1, 2 * TX, NY)),
                chosen((1, 2 * TX, NY)),
                chosen((1, 8, 2 * TX)),
            ],
            out_specs=whole((GX * BLK, NY)),
        ),
        compiler_params=params(),
        cost_estimate=cost(2.0),
        name="solve",
    )(
        place, got.reshape(8 * GY, 2 * TX), keep, cols, kink, tab["wback"], tab["t12t"],
        tab["cs"], tab["rpow"], tab["rrev"], tab["misc"], tab["rowtab"],
    )
    recv = lax.all_to_all(send.reshape(GX, BLK, NY), "gx", 0, 0, tiled=True)
    east_next, north_next, up_next, drops_out = pl.pallas_call(
        final_kernel,
        out_shape=(sds(ROWS, NY), sds(ROWS, NY), sds(ROWS, NY), sds(9, 10, CAP)),
        in_specs=[VM] * 5,
        out_specs=(VM,) * 4,
        scratch_shapes=[
            pltpu.VMEM((6 * NY, ROWS), BF16),
            pltpu.VMEM((3, ROWS, NY), F32),
            pltpu.VMEM((3, 9, CAP), F32),
        ],
        compiler_params=params(),
        cost_estimate=cost(8.0),
        name="final",
    )(recv.reshape(GX * BLK, NY), stars, tab["zback"], cell_in, state)
    fields = (
        a.reshape(NZ, NX, NY) for a in (east_next, north_next, up_next, heat_next, moist_next)
    )
    return (*fields, drops_out.reshape(3, 3, 10, CAP))


def solution(mesh):
    grid = P(None, "gx", "gy")
    blocks = P("gx", "gy", None, None)
    return jax.shard_map(
        per_device,
        mesh=mesh,
        in_specs=(grid,) * 5 + (blocks, P("gx", "gy", None), P("gx", "gy")),
        out_specs=(grid,) * 5 + (blocks,),
        check_vma=False,
    )
```

```python
import math

import jax
import jax.numpy as jnp
import numpy as np
from jax import lax
from jax.experimental import pallas as pl
from jax.experimental.pallas import tpu as pltpu
from jax.sharding import PartitionSpec as P

DT = 0.2
RELAX_TIME = 0.2
GROWTH = 0.5
CURVATURE = 0.1
SOLUTE_EFFECT = 0.05
RADIUS_FLOOR = 0.3
SATURATION_RATE = 0.1
MOIST_LOAD = 0.5
HEAT_LOAD = 1.25
ASPECT = 0.0625
HIGHEST = lax.Precision.HIGHEST

NZ = 32
NX = 8
NY = 128
GX = 16
GY = 16
TX = NX * GX
TY = NY * GY
CAP = 1024
ROWS = NZ * NX
SLOT = 12
BLK = 2 * SLOT
F32 = jnp.float32
BF16 = jnp.bfloat16


def make_tables():
    m = np.arange(NZ)
    ztab = np.cos(np.pi * m[:, None] * (2 * m[None, :] + 1) / (2 * NZ)) * np.where(
        m[:, None] == 0, math.sqrt(1.0 / NZ), math.sqrt(2.0 / NZ)
    )
    zdiff = np.zeros((NZ, NZ))
    zdiff[:-1] = (ztab.T[1:] - ztab.T[:-1]) * ASPECT
    zback = np.concatenate([ztab.T, zdiff], axis=0)
    p = np.arange(TX)

    def cas(a):
        return np.cos(a) + np.sin(a)

    w = 2 * np.pi / TX
    har = cas(w * (p[:, None] * p[None, :] % TX)) / math.sqrt(TX)
    wmain = np.zeros((2, TX, GX, 2, SLOT))
    for X in range(GX):
        for t in range(NX + 1):
            for b in range(2):
                wmain[b, :, X, b, t] = har[:, (NX * X + t) % TX]
    wmain = wmain.reshape(2 * TX, GX * BLK)
    X = np.arange(GX)
    t12 = np.concatenate(
        [cas(w * p[:, None] * NX * X[None, :]), cas(-w * p[:, None] * NX * X[None, :])], axis=0
    ) / math.sqrt(TX)
    lane = np.arange(NY)
    cosx = np.where(lane[None, :] < NX, np.cos(w * p[:, None] * lane[None, :]), 0.0)
    sinx = np.where(lane[None, :] < NX, np.sin(w * p[:, None] * lane[None, :]), 0.0)
    cs = np.concatenate([cosx, sinx], axis=0)
    lam = (
        (2 - 2 * np.cos(np.pi * m[:, None] / NZ)) + (2 - 2 * np.cos(w * p[None, :]))
    ) * ASPECT
    zero = lam <= 0
    lam = np.where(zero, 0.5, lam)
    lnr = -2.0 * np.arcsinh(np.sqrt(lam) / 2.0)
    coef = np.where(zero, 0.0, -1.0 / (2.0 * np.sinh(-lnr)))
    lnr = lnr.reshape(2, GX, TX).transpose(1, 0, 2).reshape(GX, 2 * TX)
    coef = coef.reshape(2, GX, TX).transpose(1, 0, 2).reshape(GX, 2 * TX)
    rpow = np.exp(lnr[:, :, None] * lane)
    rrev = np.exp(lnr[:, :, None] * (NY - lane))
    misc = np.zeros((GX, 2 * TX, NY))
    for k in range(8):
        misc[:, :, k] = np.exp(lnr * (1 << k))
    misc[:, :, 8] = coef
    rowtab = np.zeros((GX, 8, 2 * TX))
    rowtab[:, 0] = NY * lnr
    rowtab[:, 1] = 1.0 / (1.0 - np.exp(lnr * TY))
    absd = np.abs(lane[:, None] - lane[None, :])
    own = np.concatenate([rpow, rrev, misc, rowtab[:, :, :NY], rowtab[:, :, NY:]], axis=1)

    def f(a):
        return jnp.asarray(np.asarray(a, np.float32))

    return dict(
        ztab=f(ztab),
        zback=f(zback),
        wmain=f(wmain),
        wback=f(wmain.T),
        t12=f(t12),
        t12t=f(t12.T),
        cs=f(cs),
        own=f(own),
        absd=f(absd),
    )


def iota(shape, dim):
    return lax.broadcasted_iota(jnp.int32, shape, dim)


def dot(a, b):
    return jnp.dot(a, b, precision=HIGHEST, preferred_element_type=F32)


def field_row(fields, f, x):
    return fields[pl.ds(f * ROWS + x, NZ, stride=NX), :]


def pair_of(f0, lo, hi):
    d1, d2, d3 = (h - l for l, h in zip(lo, hi))
    s1, s2, s3 = (h + l for l, h in zip(lo, hi))
    return (45.0 * d1 - 9.0 * d2 + d3, 20.0 * f0 - 15.0 * s1 + 6.0 * s2 - s3)


def star_row(x, rows, ylo, yhi, slot, velocity, zs, lane):
    f0 = rows[x + 3]
    zs[8 : 8 + NZ, :] = f0
    zs[0:8, :] = jnp.broadcast_to(f0[0:1], (8, NY))
    zs[8 + NZ : 16 + NZ, :] = jnp.broadcast_to(f0[NZ - 1 : NZ], (8, NY))
    au, bu, av, bv, aw, bw = velocity
    a, b = pair_of(
        f0, [rows[x + 3 - k] for k in (1, 2, 3)], [rows[x + 3 + k] for k in (1, 2, 3)]
    )
    total = au * a + bu * b
    where_lo = 16 * x + 3 * slot
    halo = jnp.where(
        lane >= 64,
        pltpu.roll(ylo, (125 - where_lo) % NY, 1),
        pltpu.roll(yhi, (NY - where_lo) % NY, 1),
    )
    lo = [pltpu.roll(jnp.where(lane >= NY - k, halo, f0), k, 1) for k in (1, 2, 3)]
    hi = [pltpu.roll(jnp.where(lane < k, halo, f0), NY - k, 1) for k in (1, 2, 3)]
    a, b = pair_of(f0, lo, hi)
    total = total + (av * a + bv * b)
    a, b = pair_of(
        f0,
        [zs[8 - k : 8 - k + NZ, :] for k in (1, 2, 3)],
        [zs[8 + k : 8 + k + NZ, :] for k in (1, 2, 3)],
    )
    return f0 - (total + (aw * a + bw * b))


def velocity_rows(fields, x):
    out = []
    for f in range(3):
        a = field_row(fields, f, x) * (DT / 60.0)
        out += [a, jnp.abs(a)]
    return out


def yhalo_of(msg):
    return jnp.concatenate([msg[40:48, g * NY : (g + 1) * NY] for g in range(4)], axis=0)


def pack_blocks(out, blocks):
    for n, (drops, cells, count) in enumerate(blocks):
        out[n * SLOT : n * SLOT + 10, :] = drops
        out[n * SLOT + 10 : n * SLOT + 11, :] = cells
        out[n * SLOT + 11 : n * SLOT + 12, :] = count
    out[36:40, :] = jnp.zeros((4, CAP), F32)


def pack_kernel(
    u, v, w, h, q, drops_in, cells, counts, own, xlo, xhi, up, down, mid, fields, tabs, drops, sems
):
    copies = [
        pltpu.make_async_copy(ref, fields.at[pl.ds(f * ROWS, ROWS)], sems.at[f])
        for f, ref in enumerate((u, v, w, h, q))
    ]
    copies.append(pltpu.make_async_copy(drops_in, drops, sems.at[5]))
    copies.append(pltpu.make_async_copy(own.at[lax.axis_index("gx")], tabs, sems.at[6]))
    for copy in copies:
        copy.start()
    for copy in copies[:5]:
        copy.wait()
    for f in range(3):
        for i in range(3):
            n = f * 3 + i
            xlo[n * NZ : (n + 1) * NZ, :] = field_row(fields, f, 5 + i)
            xhi[n * NZ : (n + 1) * NZ, :] = field_row(fields, f, i)
    lane = iota((NZ, NY), 1)
    tlo = jnp.zeros((NZ, NY), F32)
    thi = jnp.zeros((NZ, NY), F32)
    for x in range(NX):
        for f in range(5):
            at = 16 * x + 3 * f
            row = field_row(fields, f, x)
            mask = (lane >= at) & (lane < at + 3)
            tlo = jnp.where(mask, pltpu.roll(row, (at - 125) % NY, 1), tlo)
            thi = jnp.where(mask, pltpu.roll(row, at, 1), thi)
    for out, tile in ((up, tlo), (down, thi)):
        for g in range(4):
            out[40:48, g * NY : (g + 1) * NY] = tile[g * 8 : (g + 1) * 8]
        out[40:48, 4 * NY :] = jnp.zeros((8, 4 * NY), F32)
    copies[5].wait()
    for s, out in ((2, up), (0, down), (1, mid)):
        for r in range(3):
            for a in range(10):
                out[r * SLOT + a : r * SLOT + a + 1, :] = drops[r, a, s : s + 1, :]
            out[r * SLOT + 10 : r * SLOT + 11, :] = cells[r, s : s + 1, :].astype(F32)
            out[r * SLOT + 11 : r * SLOT + 12, :] = jnp.full(
                (1, CAP), counts[r, s], jnp.int32
            ).astype(F32)
        out[36:40, :] = jnp.zeros((4, CAP), F32)
    copies[6].wait()


def block_of(msg, n):
    return (
        msg[n * SLOT : n * SLOT + 10, :],
        msg[n * SLOT + 10 : n * SLOT + 11, :],
        msg[n * SLOT + 11 : n * SLOT + 12, :],
    )


def relay_kernel(fields, mid, mlo, mhi, up, down):
    for out, r, x0 in ((up, 2, 5), (down, 0, 0)):
        pack_blocks(out, [block_of(mlo, r), block_of(mid, r), block_of(mhi, r)])
        for f in range(2):
            for i in range(3):
                row = field_row(fields, 3 + f, x0 + i)
                for g in range(4):
                    n = (f * 3 + i) * 4 + g
                    a, c = 40 + 8 * (n // 8), NY * (n % 8)
                    out[a : a + 8, c : c + NY] = row[g * 8 : (g + 1) * 8]


def wind_kernel(fields, xlo, xhi, mlo, mhi, ztab, after, stars, send, zs):
    lane = iota((NZ, NY), 1)
    level = iota((NZ, NY), 0)
    ylo = yhalo_of(mlo)
    yhi = yhalo_of(mhi)
    vel = [velocity_rows(fields, x) for x in range(NX)]
    for f in range(3):
        rows = [xlo[(f * 3 + i) * NZ : (f * 3 + i + 1) * NZ, :] for i in range(3)]
        rows += [field_row(fields, f, x) for x in range(NX)]
        rows += [xhi[(f * 3 + i) * NZ : (f * 3 + i + 1) * NZ, :] for i in range(3)]
        for x in range(NX):
            star = star_row(x, rows, ylo, yhi, f, vel[x], zs.at[f * NX + x], lane)
            if f == 2:
                star = jnp.where(level == NZ - 1, 0.0, star)
            at = (f * NX + x) * NZ
            stars[at : at + NZ, :] = star
    tiles = []
    ext = jnp.zeros((NZ, NY), F32)
    for x in range(NX):
        east = stars[x * NZ : (x + 1) * NZ, :]
        north = stars[(NX + x) * NZ : (NX + x + 1) * NZ, :]
        rise = stars[(2 * NX + x) * NZ : (2 * NX + x + 1) * NZ, :]
        d = east + north + rise
        if x > 0:
            d = d - stars[(x - 1) * NZ : x * NZ, :]
        d = d - jnp.where(lane == 0, 0.0, pltpu.roll(north, 1, 1))
        d = d - jnp.where(level == 0, 0.0, pltpu.roll(rise, 1, 0))
        tiles.append(d)
        ext = jnp.where(lane == x, -pltpu.roll(north, (x + 1) % NY, 1), ext)
    tiles.append(-stars[(NX - 1) * NZ : NX * NZ, :])
    tiles.append(ext)
    hat = dot(ztab[...], jnp.concatenate(tiles, axis=1))
    zeros = jnp.zeros((GX, NY), F32)
    for b in range(2):
        for t in range(SLOT):
            if t < NX + 2:
                val = hat[b * GX : (b + 1) * GX, t * NY : (t + 1) * NY]
            else:
                val = zeros
            send[pl.ds(b * SLOT + t, GX, stride=BLK), :] = val


def own_tables(tabs):
    n = 2 * TX
    return tabs.at[0:n], tabs.at[n : 2 * n], tabs.at[2 * n : 3 * n], tabs.at[3 * n : 3 * n + 16]


def scan_kernel(recv, wmain, t12, cs, tabs, absd, after, msg, keep, cols, kink):
    rpow, rrev, misc, rowtab = own_tables(tabs)
    lane = iota((2 * TX, NY), 1)
    d = dot(wmain[...], recv[...])
    ends = []
    for b in range(2):
        e16 = recv[pl.ds(b * SLOT + NX + 1, GX, stride=BLK), :]
        prod = dot(t12[...], e16) * cs[...]
        ends.append(jnp.sum(prod[:TX] + prod[TX:], axis=1, keepdims=True))
    e = jnp.concatenate(ends, axis=0)
    fwd = d
    bwd = d
    for k in range(7):
        s = 1 << k
        a = jnp.broadcast_to(misc[:, k : k + 1], (2 * TX, NY))
        fwd = fwd + jnp.where(lane >= s, a * pltpu.roll(fwd, s, 1), 0.0)
        bwd = bwd + jnp.where(lane < NY - s, a * pltpu.roll(bwd, NY - s, 1), 0.0)
    r1 = misc[:, 0:1]
    r128 = misc[:, 7:8]
    out_right = r1 * fwd[:, NY - 1 : NY] + e
    out_left = bwd[:, 0:1] + r128 * e
    keep[...] = fwd + bwd - d + rrev[...] * e
    table = jnp.where(lane == 0, out_right, jnp.where(lane == 1, out_left, 0.0))
    d8 = d[0:8]
    e8 = e[0:8]
    lane8 = iota((8, NY), 1)
    lanef = lane8.astype(F32)
    s0 = jnp.sum(d8, axis=1, keepdims=True) + e8
    s1 = jnp.sum(d8 * lanef, axis=1, keepdims=True) + float(NY) * e8
    top = jnp.where(lane8 == 2, s0, jnp.where(lane8 == 3, s1, table[0:8]))
    table = jnp.concatenate([top, table[8:]], axis=0)
    cols[...] = table
    turned = table.T[0:8]
    for y in range(GY):
        msg[y * 8 : (y + 1) * 8, :] = turned
    kink[...] = dot(d8, absd[...]) + e8 * (float(NY) - lanef)


def solve_kernel(got, keep, cols, kink, wback, t12t, cs, tabs, after, send):
    rpow, rrev, misc, rowtab = own_tables(tabs)
    here = lax.axis_index("gy")
    first = (lax.axis_index("gx") == 0).astype(F32)
    who = iota((GY, 2 * TX), 0)
    all_right = jnp.concatenate([got[y * 8 : y * 8 + 1, :] for y in range(GY)], axis=0)
    all_left = jnp.concatenate([got[y * 8 + 1 : y * 8 + 2, :] for y in range(GY)], axis=0)
    s0 = jnp.concatenate([got[y * 8 + 2 : y * 8 + 3, 0:1] for y in range(GY)], axis=0)
    s1 = jnp.concatenate([got[y * 8 + 3 : y * 8 + 4, 0:1] for y in range(GY)], axis=0)
    lnr = jnp.concatenate([rowtab[0:1, :], rowtab[8:9, :]], axis=1)
    inv = jnp.concatenate([rowtab[1:2, :], rowtab[9:10, :]], axis=1)
    after = ((here - who - 1) & (GY - 1)).astype(F32)
    before = ((who - here - 1) & (GY - 1)).astype(F32)
    in_left = jnp.sum(jnp.exp(after * lnr) * all_right, axis=0, keepdims=True) * inv
    in_right = jnp.sum(jnp.exp(before * lnr) * all_left, axis=0, keepdims=True) * inv
    row = iota((8, 2 * TX), 0)
    turned = jnp.where(row == 0, in_left, jnp.where(row == 1, in_right, 0.0)).T
    in_left = turned[:, 0:1]
    in_right = turned[:, 1:2]
    coef = misc[:, 8:9]
    pres = coef * (keep[...] + rpow[...] * in_left + rrev[...] * in_right)
    edge = coef * (cols[:, 0:1] + misc[:, 7:8] * in_left + in_right)
    who1 = iota((GY, 1), 0)
    far = (NY * ((here - who1) & (GY - 1))).astype(F32)
    mine = who1 == here
    sum0 = jnp.sum(s0, axis=0, keepdims=True)
    own0 = jnp.sum(jnp.where(mine, s0, 0.0), axis=0, keepdims=True)
    own1 = jnp.sum(jnp.where(mine, s1, 0.0), axis=0, keepdims=True)
    lin = 0.5 * (sum0 - own0) + jnp.sum(s1 - far * s0, axis=0, keepdims=True) * (1.0 / TY)
    quad = sum0 * (0.5 / TY)
    lanef = iota((8, NY), 1).astype(F32)
    top = 0.5 * kink[...] + lanef * (lin - lanef * quad)
    edge0 = 0.5 * (float(NY) * own0 - own1) + float(NY) * (lin - float(NY) * quad)
    row8 = iota((8, NY), 0)
    top = pres[0:8] + jnp.where(row8 == 0, first * top, 0.0)
    pres = jnp.concatenate([top, pres[8:]], axis=0)
    row1 = iota((2 * TX, 1), 0)
    edge = edge + jnp.where(row1 == 0, first * edge0, 0.0)
    send[...] = dot(wback[...], pres)
    for b in range(2):
        eb = edge[b * TX : (b + 1) * TX]
        spread = jnp.concatenate([cs[0:TX, :] * eb, cs[TX:, :] * eb], axis=0)
        send[pl.ds(b * SLOT + NX + 1, GX, stride=BLK), :] = dot(t12t[...], spread)


def store_table(lhs, n, table):
    turned = table.T
    hi = turned.astype(BF16)
    lhs[n * NY : (n + 1) * NY, 0:ROWS] = hi
    lhs[n * NY : (n + 1) * NY, ROWS:] = (turned - hi.astype(F32)).astype(BF16)


def masks_of(cells):
    width = cells.shape[1]
    rowid = ((cells >> 7) & (NX - 1)) * NZ + (cells >> 10)
    hot = jnp.where(iota((ROWS, width), 0) == rowid, 1.0, 0.0).astype(BF16)
    pick = iota((NY, width), 0) == (cells & (NY - 1))
    return hot, pick


def gather_one(lhs, n, hot, pick):
    both = jnp.concatenate([hot, hot], axis=0)
    got = jnp.dot(lhs[n * NY : (n + 1) * NY, :], both, preferred_element_type=F32)
    return jnp.sum(jnp.where(pick, got, 0.0), axis=0, keepdims=True)


CHUNK = 512


def heat_kernel(fields, mid, mlo, mhi, clo, chi, after, stars, lhs, cell_out, state, zs):
    lane = iota((NZ, NY), 1)
    ylo = yhalo_of(mlo)
    yhi = yhalo_of(mhi)
    vel = [velocity_rows(fields, x) for x in range(NX)]

    def side(msg, n):
        parts = []
        for g in range(4):
            k = n * 4 + g
            a, c = 40 + 8 * (k // 8), NY * (k % 8)
            parts.append(msg[a : a + 8, c : c + NY])
        return jnp.concatenate(parts, axis=0)

    for f in range(2):
        rows = [side(clo, f * 3 + i) for i in range(3)]
        rows += [field_row(fields, 3 + f, x) for x in range(NX)]
        rows += [side(chi, f * 3 + i) for i in range(3)]
        for x in range(NX):
            star = star_row(x, rows, ylo, yhi, 3 + f, vel[x], zs.at[f * NX + x], lane)
            at = (f * NX + x) * NZ
            stars[at : at + NZ, :] = star
        store_table(lhs, f, stars[f * ROWS : (f + 1) * ROWS, :])
    for r in range(3):
        for s in range(3):
            n = r * 3 + s
            if r == 0:
                block = block_of(clo, s)
            elif r == 2:
                block = block_of(chi, s)
            else:
                block = block_of((mlo, mid, mhi)[s], 1)
            values, cell, count = block
            for a in range(10):
                state[a, n : n + 1, :] = values[a : a + 1]
            cell_out[n : n + 1, :] = cell.astype(jnp.int32)
            slot = iota((1, CAP), 1).astype(F32)
            state[10, n : n + 1, :] = jnp.where(slot < count, 1.0, 0.0)


def growth_kernel(lhs, cell, state, after, state_out, gain_out, air):
    def gather_block(n, carry):
        for c in range(CAP // CHUNK):
            at = c * CHUNK
            hot, pick = masks_of(cell[pl.ds(n, 1), at : at + CHUNK])
            for f in range(2):
                air[f, pl.ds(n, 1), at : at + CHUNK] = gather_one(lhs, f, hot, pick)
        return carry

    lax.fori_loop(0, 9, gather_block, 0)
    live = state[10]
    radius = state[6]
    cubed = radius * radius * radius
    keeping = jnp.exp(-DT / (RELAX_TIME * radius * radius))
    saturation = air[1] * jnp.exp(-SATURATION_RATE * air[0]) - 1.0
    squared = radius * radius + GROWTH * (
        saturation - CURVATURE / radius + SOLUTE_EFFECT * state[8] / cubed
    )
    new_radius = jnp.sqrt(jnp.maximum(squared, RADIUS_FLOOR * RADIUS_FLOOR))
    gain_out[...] = live * state[7] * (new_radius * new_radius * new_radius - cubed)
    state_out[6] = new_radius * live
    state_out[7] = state[7] * live
    state_out[8] = state[8] * live
    state_out[9] = (state[9] + DT) * live
    for a in range(3):
        state_out[a] = state[a] * live
        state_out[3 + a] = state[3 + a] * (keeping * live)
    state_out[10] = (1.0 - keeping) * live


def scatter_kernel(stars, cell, gain, after, heat_next, moist_next, acc):
    acc[...] = jnp.zeros_like(acc)

    def scatter_block(n, carry):
        for c in range(CAP // CHUNK):
            at = c * CHUNK
            hot, pick = masks_of(cell[pl.ds(n, 1), at : at + CHUNK])
            g = gain[pl.ds(n, 1), at : at + CHUNK]
            hi = g.astype(BF16).astype(F32)
            lo = g - hi
            z = jnp.concatenate(
                [
                    jnp.where(pick, hi, 0.0).astype(BF16),
                    jnp.where(pick, lo, 0.0).astype(BF16),
                ],
                axis=0,
            )
            acc[...] += lax.dot_general(
                hot, z, (((1,), (1,)), ((), ())), preferred_element_type=F32
            )
        return carry

    lax.fori_loop(0, 9, scatter_block, 0)
    for x in range(NX):
        a = x * NZ
        condensed = acc[a : a + NZ, 0:NY] + acc[a : a + NZ, NY:]
        heat_next[pl.ds(x, NZ, stride=NX), :] = stars[a : a + NZ, :] + HEAT_LOAD * condensed
        moist_next[pl.ds(x, NZ, stride=NX), :] = (
            stars[ROWS + a : ROWS + a + NZ, :] - MOIST_LOAD * condensed
        )


def final_kernel(
    recv, stars, zback, cell, state, east_next, north_next, up_next, drops_out, lhs, next_rows, air
):
    lane = iota((NZ, NY), 1)
    tiles = []
    for t in range(NX + 2):
        tiles.append(
            jnp.concatenate(
                [recv[pl.ds(b * SLOT + t, GX, stride=BLK), :] for b in range(2)], axis=0
            )
        )
    both = dot(zback[...], jnp.concatenate(tiles, axis=1))
    pres = [both[:NZ, t * NY : (t + 1) * NY] for t in range(NX + 2)]
    edge = pres[NX + 1]
    for x in range(NX):
        east = stars[x * NZ : (x + 1) * NZ, :] - (pres[x + 1] - pres[x]) * ASPECT
        ahead = pltpu.roll(
            jnp.where(lane == 0, pltpu.roll(edge, (NY - x) % NY, 1), pres[x]), NY - 1, 1
        )
        north = stars[(NX + x) * NZ : (NX + x + 1) * NZ, :] - (ahead - pres[x])
        rise = (
            stars[(2 * NX + x) * NZ : (2 * NX + x + 1) * NZ, :]
            - both[NZ:, x * NY : (x + 1) * NY]
        )
        for f, (val, ref) in enumerate(
            ((east, east_next), (north, north_next), (rise, up_next))
        ):
            ref[pl.ds(x, NZ, stride=NX), :] = val
            next_rows[f, x * NZ : (x + 1) * NZ, :] = val
    for f in range(3):
        store_table(lhs, f, next_rows[f])

    def gather_block(n, carry):
        for c in range(CAP // CHUNK):
            at = c * CHUNK
            hot, pick = masks_of(cell[pl.ds(n, 1), at : at + CHUNK])
            for f in range(3):
                air[f, pl.ds(n, 1), at : at + CHUNK] = gather_one(lhs, f, hot, pick)
        return carry

    lax.fori_loop(0, 9, gather_block, 0)
    mix = state[10]
    for a in range(3):
        speed = air[a] * mix + state[3 + a]
        offset = state[a] + DT * speed
        for r in range(3):
            drops_out[r, 3 + a] = speed[3 * r : 3 * r + 3]
            drops_out[r, a] = offset[3 * r : 3 * r + 3]
    for a in range(6, 10):
        for r in range(3):
            drops_out[r, a] = state[a, 3 * r : 3 * r + 3, :]


VM = pl.BlockSpec(memory_space=pltpu.VMEM)
SM = pl.BlockSpec(memory_space=pltpu.SMEM)
ANY = pl.BlockSpec(memory_space=pl.ANY)
HBM = pl.BlockSpec(memory_space=pltpu.HBM)


def sds(*shape, dtype=F32):
    return jax.ShapeDtypeStruct(shape, dtype)


def call(kernel, name, us, out_shape, in_specs, scratch=(), mib=12):
    return pl.pallas_call(
        kernel,
        out_shape=out_shape,
        in_specs=in_specs,
        out_specs=tuple(VM for _ in out_shape),
        scratch_shapes=list(scratch),
        compiler_params=pltpu.CompilerParams(vmem_limit_bytes=mib * 1024 * 1024),
        cost_estimate=pl.CostEstimate(
            flops=int(us * 5e8), bytes_accessed=int(us * 2e6), transcendentals=0
        ),
        name=name,
    )


def ring(axis, shift):
    count = lax.axis_size(axis)
    return [(i, (i + shift) % count) for i in range(count)]


def per_device(u, v, w, h, q, droplets, cells, counts):
    tab = make_tables()
    u, v, w, h, q = (a.reshape(ROWS, NY) for a in (u, v, w, h, q))
    drops = droplets.transpose(0, 2, 1, 3)
    xlo, xhi, up, down, mid, fields, tabs = call(
        pack_kernel,
        "pack",
        2.5,
        (
            sds(9 * NZ, NY), sds(9 * NZ, NY), sds(48, CAP), sds(48, CAP), sds(40, CAP),
            sds(5 * ROWS, NY), sds(6 * TX + 16, NY),
        ),
        [HBM] * 6 + [VM, SM, HBM],
        [pltpu.VMEM((3, 10, 3, CAP), F32), pltpu.SemaphoreType.DMA((7,))],
    )(u, v, w, h, q, drops, cells, counts, tab["own"])
    mlo = lax.ppermute(up, "gy", ring("gy", 1))
    mhi = lax.ppermute(down, "gy", ring("gy", -1))
    xlo = lax.ppermute(xlo, "gx", ring("gx", 1))
    xhi = lax.ppermute(xhi, "gx", ring("gx", -1))
    cup, cdown = call(
        relay_kernel, "relay", 1.0, (sds(64, CAP), sds(64, CAP)), [VM] * 4
    )(fields, mid, mlo, mhi)
    clo = lax.ppermute(cup, "gx", ring("gx", 1))
    chi = lax.ppermute(cdown, "gx", ring("gx", -1))
    stars, send = call(
        wind_kernel,
        "winds",
        3.0,
        (sds(3 * ROWS, NY), sds(GX * BLK, NY)),
        [VM] * 6 + [ANY],
        [pltpu.VMEM((3 * NX, NZ + 16, NY), F32)],
    )(fields, xlo, xhi, mlo, mhi, tab["ztab"], cup)
    recv = lax.all_to_all(send.reshape(GX, BLK, NY), "gx", 0, 0, tiled=True)
    stars_hq, lhs, cell_in, state = call(
        heat_kernel,
        "heat",
        3.0,
        (
            sds(2 * ROWS, NY), sds(2 * NY, 2 * ROWS, dtype=BF16),
            sds(9, CAP, dtype=jnp.int32), sds(11, 9, CAP),
        ),
        [VM] * 6 + [ANY],
        [pltpu.VMEM((2 * NX, NZ + 16, NY), F32)],
    )(fields, mid, mlo, mhi, clo, chi, stars)
    msg, keep, cols, kink = call(
        scan_kernel,
        "scan",
        2.0,
        (sds(8 * GY, 2 * TX), sds(2 * TX, NY), sds(2 * TX, NY), sds(8, NY)),
        [VM] * 6 + [ANY],
    )(
        recv.reshape(GX * BLK, NY), tab["wmain"], tab["t12"], tab["cs"], tabs, tab["absd"], state
    )
    got = lax.all_to_all(msg.reshape(GY, 8, 2 * TX), "gy", 0, 0, tiled=True)
    state, gain = call(
        growth_kernel,
        "growth",
        5.0,
        (sds(11, 9, CAP), sds(9, CAP)),
        [VM] * 3 + [ANY],
        [pltpu.VMEM((2, 9, CAP), F32)],
    )(lhs, cell_in, state, keep)
    (send,) = call(
        solve_kernel, "solve", 2.0, (sds(GX * BLK, NY),), [VM] * 8 + [ANY]
    )(
        got.reshape(8 * GY, 2 * TX), keep, cols, kink, tab["wback"], tab["t12t"], tab["cs"], tabs,
        gain,
    )
    recv = lax.all_to_all(send.reshape(GX, BLK, NY), "gx", 0, 0, tiled=True)
    heat_next, moist_next = call(
        scatter_kernel,
        "scatter",
        4.0,
        (sds(ROWS, NY), sds(ROWS, NY)),
        [VM] * 3 + [ANY],
        [pltpu.VMEM((ROWS, 2 * NY), F32)],
    )(stars_hq, cell_in, gain, send)
    east_next, north_next, up_next, drops_out = call(
        final_kernel,
        "final",
        8.0,
        (sds(ROWS, NY), sds(ROWS, NY), sds(ROWS, NY), sds(3, 10, 3, CAP)),
        [VM] * 5,
        [
            pltpu.VMEM((3 * NY, 2 * ROWS), BF16),
            pltpu.VMEM((3, ROWS, NY), F32),
            pltpu.VMEM((3, 9, CAP), F32),
        ],
    )(recv.reshape(GX * BLK, NY), stars, tab["zback"], cell_in, state)
    out = (
        a.reshape(NZ, NX, NY) for a in (east_next, north_next, up_next, heat_next, moist_next)
    )
    return (*out, drops_out.transpose(0, 2, 1, 3))


def solution(mesh):
    grid = P(None, "gx", "gy")
    blocks = P("gx", "gy", None, None)
    return jax.shard_map(
        per_device,
        mesh=mesh,
        in_specs=(grid,) * 5 + (blocks, P("gx", "gy", None), P("gx", "gy")),
        out_specs=(grid,) * 5 + (blocks,),
        check_vma=False,
    )
```

```python
import math

import jax
import jax.numpy as jnp
import numpy as np
from jax import lax
from jax.experimental import pallas as pl
from jax.experimental.pallas import tpu as pltpu
from jax.sharding import PartitionSpec as P

DT = 0.2
RELAX_TIME = 0.2
GROWTH = 0.5
CURVATURE = 0.1
SOLUTE_EFFECT = 0.05
RADIUS_FLOOR = 0.3
SATURATION_RATE = 0.1
MOIST_LOAD = 0.5
HEAT_LOAD = 1.25
ASPECT = 0.0625
HIGHEST = lax.Precision.HIGHEST

NZ = 32
NX = 8
NY = 128
GX = 16
GY = 16
TX = NX * GX
TY = NY * GY
CAP = 1024
ROWS = NZ * NX
SLOT = 12
BLK = 2 * SLOT
F32 = jnp.float32
BF16 = jnp.bfloat16


def make_tables():
    m = np.arange(NZ)
    ztab = np.cos(np.pi * m[:, None] * (2 * m[None, :] + 1) / (2 * NZ)) * np.where(
        m[:, None] == 0, math.sqrt(1.0 / NZ), math.sqrt(2.0 / NZ)
    )
    zdiff = np.zeros((NZ, NZ))
    zdiff[:-1] = (ztab.T[1:] - ztab.T[:-1]) * ASPECT
    zback = np.concatenate([ztab.T, zdiff], axis=0)
    p = np.arange(TX)

    def cas(a):
        return np.cos(a) + np.sin(a)

    w = 2 * np.pi / TX
    har = cas(w * (p[:, None] * p[None, :] % TX)) / math.sqrt(TX)
    wmain = np.zeros((2, TX, GX, 2, SLOT))
    for X in range(GX):
        for t in range(NX + 1):
            for b in range(2):
                wmain[b, :, X, b, t] = har[:, (NX * X + t) % TX]
    wmain = wmain.reshape(2 * TX, GX * BLK)
    X = np.arange(GX)
    t12 = np.concatenate(
        [cas(w * p[:, None] * NX * X[None, :]), cas(-w * p[:, None] * NX * X[None, :])], axis=0
    ) / math.sqrt(TX)
    lane = np.arange(NY)
    cosx = np.where(lane[None, :] < NX, np.cos(w * p[:, None] * lane[None, :]), 0.0)
    sinx = np.where(lane[None, :] < NX, np.sin(w * p[:, None] * lane[None, :]), 0.0)
    cs = np.concatenate([cosx, sinx], axis=0)
    lam = (
        (2 - 2 * np.cos(np.pi * m[:, None] / NZ)) + (2 - 2 * np.cos(w * p[None, :]))
    ) * ASPECT
    zero = lam <= 0
    lam = np.where(zero, 0.5, lam)
    lnr = -2.0 * np.arcsinh(np.sqrt(lam) / 2.0)
    coef = np.where(zero, 0.0, -1.0 / (2.0 * np.sinh(-lnr)))
    lnr = lnr.reshape(2, GX, TX).transpose(1, 0, 2).reshape(GX, 2 * TX)
    coef = coef.reshape(2, GX, TX).transpose(1, 0, 2).reshape(GX, 2 * TX)
    rpow = np.exp(lnr[:, :, None] * lane)
    rrev = np.exp(lnr[:, :, None] * (NY - lane))
    misc = np.zeros((GX, 2 * TX, NY))
    for k in range(8):
        misc[:, :, k] = np.exp(lnr * (1 << k))
    misc[:, :, 8] = coef
    rowtab = np.zeros((GX, 8, 2 * TX))
    rowtab[:, 0] = NY * lnr
    rowtab[:, 1] = 1.0 / (1.0 - np.exp(lnr * TY))
    own = np.concatenate([rpow, rrev, misc, rowtab[:, :, :NY], rowtab[:, :, NY:]], axis=1)

    def f(a):
        return jnp.asarray(np.asarray(a, np.float32))

    return dict(
        ztab=f(ztab),
        zback=f(zback),
        wmain=f(wmain),
        wback=f(wmain.T),
        t12=f(t12),
        t12t=f(t12.T),
        cs=f(cs),
        own=f(own),
    )


def iota(shape, dim):
    return lax.broadcasted_iota(jnp.int32, shape, dim)


def dot(a, b):
    return jnp.dot(a, b, precision=HIGHEST, preferred_element_type=F32)


def field_row(fields, f, x):
    return fields[pl.ds(f * ROWS + x, NZ, stride=NX), :]


def pair_of(f0, lo, hi):
    d1, d2, d3 = (h - l for l, h in zip(lo, hi))
    s1, s2, s3 = (h + l for l, h in zip(lo, hi))
    return (45.0 * d1 - 9.0 * d2 + d3, 20.0 * f0 - 15.0 * s1 + 6.0 * s2 - s3)


def star_row(x, rows, ylo, yhi, slot, velocity, zs, lane):
    f0 = rows[x + 3]
    zs[8 : 8 + NZ, :] = f0
    zs[0:8, :] = jnp.broadcast_to(f0[0:1], (8, NY))
    zs[8 + NZ : 16 + NZ, :] = jnp.broadcast_to(f0[NZ - 1 : NZ], (8, NY))
    au, bu, av, bv, aw, bw = velocity
    a, b = pair_of(
        f0, [rows[x + 3 - k] for k in (1, 2, 3)], [rows[x + 3 + k] for k in (1, 2, 3)]
    )
    total = au * a + bu * b
    where_lo = 16 * x + 3 * slot
    halo = jnp.where(
        lane >= 64,
        pltpu.roll(ylo, (125 - where_lo) % NY, 1),
        pltpu.roll(yhi, (NY - where_lo) % NY, 1),
    )
    lo = [pltpu.roll(jnp.where(lane >= NY - k, halo, f0), k, 1) for k in (1, 2, 3)]
    hi = [pltpu.roll(jnp.where(lane < k, halo, f0), NY - k, 1) for k in (1, 2, 3)]
    a, b = pair_of(f0, lo, hi)
    total = total + (av * a + bv * b)
    a, b = pair_of(
        f0,
        [zs[8 - k : 8 - k + NZ, :] for k in (1, 2, 3)],
        [zs[8 + k : 8 + k + NZ, :] for k in (1, 2, 3)],
    )
    return f0 - (total + (aw * a + bw * b))


def velocity_rows(fields, x):
    out = []
    for f in range(3):
        a = field_row(fields, f, x) * (DT / 60.0)
        out += [a, jnp.abs(a)]
    return out


def sides_kernel(u, v, w, h, q, xlo, xhi, ylo, yhi, done, fields, sems):
    done[...] = jnp.zeros_like(done)
    copies = [
        pltpu.make_async_copy(ref, fields.at[pl.ds(f * ROWS, ROWS)], sems.at[f])
        for f, ref in enumerate((u, v, w, h, q))
    ]
    for copy in copies:
        copy.start()
    for copy in copies:
        copy.wait()
    for f in range(3):
        for i in range(3):
            n = f * 3 + i
            xlo[n * NZ : (n + 1) * NZ, :] = field_row(fields, f, 5 + i)
            xhi[n * NZ : (n + 1) * NZ, :] = field_row(fields, f, i)
    lane = iota((NZ, NY), 1)
    tlo = jnp.zeros((NZ, NY), F32)
    thi = jnp.zeros((NZ, NY), F32)
    for x in range(NX):
        for f in range(5):
            at = 16 * x + 3 * f
            row = field_row(fields, f, x)
            mask = (lane >= at) & (lane < at + 3)
            tlo = jnp.where(mask, pltpu.roll(row, (at - 125) % NY, 1), tlo)
            thi = jnp.where(mask, pltpu.roll(row, at, 1), thi)
    ylo[0:NZ, :] = tlo
    yhi[0:NZ, :] = thi
    ylo[NZ:, :] = jnp.zeros((8 * NZ, NY), F32)
    yhi[NZ:, :] = jnp.zeros((8 * NZ, NY), F32)


def pack_kernel(
    u, v, w, h, q, drops_in, cells, counts, own, after,
    up, down, mid, part, fields, tabs, drops, sems,
):
    copies = [
        pltpu.make_async_copy(ref, fields.at[pl.ds(f * ROWS, ROWS)], sems.at[f])
        for f, ref in enumerate((u, v, w, h, q))
    ]
    copies.append(pltpu.make_async_copy(drops_in, drops, sems.at[5]))
    copies.append(pltpu.make_async_copy(own.at[lax.axis_index("gx")], tabs, sems.at[6]))
    for copy in copies:
        copy.start()
    copies[5].wait()
    for out, at, r, s in (
        [(up, r * SLOT, r, 2) for r in range(3)]
        + [(down, r * SLOT, r, 0) for r in range(3)]
        + [(mid, 0, 1, 1), (part, 0, 2, 1), (part, 40, 0, 1)]
    ):
        for a in range(10):
            out[at + a : at + a + 1, :] = drops[r, a, s : s + 1, :]
        out[at + 10 : at + 11, :] = cells[r, s : s + 1, :].astype(F32)
        out[at + 11 : at + 12, :] = jnp.full((1, CAP), counts[r, s], jnp.int32).astype(F32)
    for out, at, rows in ((up, 36, 4), (down, 36, 4), (mid, 12, 4), (part, 12, 4), (part, 52, 4)):
        out[at : at + rows, :] = jnp.zeros((rows, CAP), F32)
    copies[3].wait()
    copies[4].wait()
    for k, x0 in enumerate((5, 0)):
        for f in range(2):
            for i in range(3):
                row = field_row(fields, 3 + f, x0 + i)
                for g in range(4):
                    n = (f * 3 + i) * 4 + g
                    a, c = 40 * k + 16 + 8 * (n // 8), NY * (n % 8)
                    part[a : a + 8, c : c + NY] = row[g * 8 : (g + 1) * 8]
    for k in (0, 1, 2, 6):
        copies[k].wait()


def block_of(msg, n):
    return (
        msg[n * SLOT : n * SLOT + 10, :],
        msg[n * SLOT + 10 : n * SLOT + 11, :],
        msg[n * SLOT + 11 : n * SLOT + 12, :],
    )


def relay_kernel(part, mlo, mhi, after, up, down, done):
    done[...] = jnp.zeros_like(done)
    for n, (out, r) in enumerate(((up, 2), (down, 0))):
        out[0:12, :] = mlo[r * SLOT : (r + 1) * SLOT, :]
        out[12:24, :] = mhi[r * SLOT : (r + 1) * SLOT, :]
        out[24:64, :] = part[n * 40 : (n + 1) * 40, :]


def wind_kernel(fields, xlo, xhi, ylo_in, yhi_in, ztab, east_s, north_s, rise_s, send, done, zs):
    done[...] = jnp.zeros_like(done)
    lane = iota((NZ, NY), 1)
    level = iota((NZ, NY), 0)
    ylo = ylo_in[0:NZ, :]
    yhi = yhi_in[0:NZ, :]
    vel = [velocity_rows(fields, x) for x in range(NX)]
    for f in range(3):
        rows = [xlo[(f * 3 + i) * NZ : (f * 3 + i + 1) * NZ, :] for i in range(3)]
        rows += [field_row(fields, f, x) for x in range(NX)]
        rows += [xhi[(f * 3 + i) * NZ : (f * 3 + i + 1) * NZ, :] for i in range(3)]
        for x in range(NX):
            star = star_row(x, rows, ylo, yhi, f, vel[x], zs.at[f * NX + x], lane)
            if f == 2:
                star = jnp.where(level == NZ - 1, 0.0, star)
            (east_s, north_s, rise_s)[f][pl.ds(x, NZ, stride=NX), :] = star
    tiles = []
    ext = jnp.zeros((NZ, NY), F32)
    for x in range(NX):
        east = field_row(east_s, 0, x)
        north = field_row(north_s, 0, x)
        rise = field_row(rise_s, 0, x)
        d = east + north + rise
        if x > 0:
            d = d - field_row(east_s, 0, x - 1)
        d = d - jnp.where(lane == 0, 0.0, pltpu.roll(north, 1, 1))
        d = d - jnp.where(level == 0, 0.0, pltpu.roll(rise, 1, 0))
        tiles.append(d)
        ext = jnp.where(lane == x, -pltpu.roll(north, (x + 1) % NY, 1), ext)
    tiles.append(-field_row(east_s, 0, NX - 1))
    tiles.append(ext)
    hat = dot(ztab[...], jnp.concatenate(tiles, axis=1))
    zeros = jnp.zeros((GX, NY), F32)
    for b in range(2):
        for t in range(SLOT):
            if t < NX + 2:
                val = hat[b * GX : (b + 1) * GX, t * NY : (t + 1) * NY]
            else:
                val = zeros
            send[pl.ds(b * SLOT + t, GX, stride=BLK), :] = val


def own_tables(tabs):
    n = 2 * TX
    return tabs.at[0:n], tabs.at[n : 2 * n], tabs.at[2 * n : 3 * n], tabs.at[3 * n : 3 * n + 16]


def scan_kernel(recv, wmain, t12, cs, tabs, after, msg, keep, kink, done):
    done[...] = jnp.zeros_like(done)
    rpow, rrev, misc, rowtab = own_tables(tabs)
    lane = iota((2 * TX, NY), 1)
    d = dot(wmain[...], recv[...])
    ends = []
    for b in range(2):
        e16 = recv[pl.ds(b * SLOT + NX + 1, GX, stride=BLK), :]
        prod = dot(t12[...], e16) * cs[...]
        ends.append(jnp.sum(prod[:TX] + prod[TX:], axis=1, keepdims=True))
    e = jnp.concatenate(ends, axis=0)
    fwd = d
    bwd = d
    for k in range(7):
        s = 1 << k
        a = jnp.broadcast_to(misc[:, k : k + 1], (2 * TX, NY))
        fwd = fwd + jnp.where(lane >= s, a * pltpu.roll(fwd, s, 1), 0.0)
        bwd = bwd + jnp.where(lane < NY - s, a * pltpu.roll(bwd, NY - s, 1), 0.0)
    r1 = misc[:, 0:1]
    r128 = misc[:, 7:8]
    out_right = r1 * fwd[:, NY - 1 : NY] + e
    out_left = bwd[:, 0:1] + r128 * e
    keep[...] = fwd + bwd - d + rrev[...] * e
    lane1 = lane[:TX]
    table = jnp.zeros((TX, NY), F32)
    for b in range(2):
        table = jnp.where(lane1 == b, out_right[b * TX : (b + 1) * TX], table)
        table = jnp.where(lane1 == 2 + b, out_left[b * TX : (b + 1) * TX], table)
    d8 = d[0:8]
    e8 = e[0:8]
    lane8 = iota((8, NY), 1)
    lanef = lane8.astype(F32)
    s0 = jnp.sum(d8, axis=1, keepdims=True) + e8
    s1 = jnp.sum(d8 * lanef, axis=1, keepdims=True) + float(NY) * e8
    top = jnp.where(lane8 == 4, s0, jnp.where(lane8 == 5, s1, table[0:8]))
    table = jnp.concatenate([top, table[8:]], axis=0)
    turned = table.T[0:8]
    for y in range(GY):
        msg[y * 8 : (y + 1) * 8, :] = turned
    apart = jnp.abs(iota((NY, NY), 0) - iota((NY, NY), 1)).astype(F32)
    kink[...] = dot(d8, apart) + e8 * (float(NY) - lanef)


def solve_kernel(got, keep, kink, wback, t12t, cs, tabs, after, send, done):
    done[...] = jnp.zeros_like(done)
    rpow, rrev, misc, rowtab = own_tables(tabs)
    here = lax.axis_index("gy")
    first = (lax.axis_index("gx") == 0).astype(F32)
    who = iota((GY, 2 * TX), 0)
    def rows(k):
        return jnp.concatenate([got[y * 8 + k : y * 8 + k + 1, :] for y in range(GY)], axis=0)

    all_right = jnp.concatenate([rows(0), rows(1)], axis=1)
    all_left = jnp.concatenate([rows(2), rows(3)], axis=1)
    s0 = rows(4)[:, 0:1]
    s1 = rows(5)[:, 0:1]
    lnr = jnp.concatenate([rowtab[0:1, :], rowtab[8:9, :]], axis=1)
    inv = jnp.concatenate([rowtab[1:2, :], rowtab[9:10, :]], axis=1)
    after = ((here - who - 1) & (GY - 1)).astype(F32)
    before = ((who - here - 1) & (GY - 1)).astype(F32)
    in_left = jnp.sum(jnp.exp(after * lnr) * all_right, axis=0, keepdims=True) * inv
    in_right = jnp.sum(jnp.exp(before * lnr) * all_left, axis=0, keepdims=True) * inv
    own_right = jnp.sum(jnp.where(who == here, all_right, 0.0), axis=0, keepdims=True)
    row = iota((8, 2 * TX), 0)
    turned = jnp.where(row == 0, in_left, jnp.where(row == 1, in_right, own_right)).T
    in_left = turned[:, 0:1]
    in_right = turned[:, 1:2]
    coef = misc[:, 8:9]
    pres = coef * (keep[...] + rpow[...] * in_left + rrev[...] * in_right)
    edge = coef * (turned[:, 2:3] + misc[:, 7:8] * in_left + in_right)
    who1 = iota((GY, 1), 0)
    far = (NY * ((here - who1) & (GY - 1))).astype(F32)
    mine = who1 == here
    sum0 = jnp.sum(s0, axis=0, keepdims=True)
    own0 = jnp.sum(jnp.where(mine, s0, 0.0), axis=0, keepdims=True)
    own1 = jnp.sum(jnp.where(mine, s1, 0.0), axis=0, keepdims=True)
    lin = 0.5 * (sum0 - own0) + jnp.sum(s1 - far * s0, axis=0, keepdims=True) * (1.0 / TY)
    quad = sum0 * (0.5 / TY)
    lanef = iota((8, NY), 1).astype(F32)
    top = 0.5 * kink[...] + lanef * (lin - lanef * quad)
    edge0 = 0.5 * (float(NY) * own0 - own1) + float(NY) * (lin - float(NY) * quad)
    row8 = iota((8, NY), 0)
    top = pres[0:8] + jnp.where(row8 == 0, first * top, 0.0)
    pres = jnp.concatenate([top, pres[8:]], axis=0)
    row1 = iota((2 * TX, 1), 0)
    edge = edge + jnp.where(row1 == 0, first * edge0, 0.0)
    send[...] = dot(wback[...], pres)
    for b in range(2):
        eb = edge[b * TX : (b + 1) * TX]
        spread = jnp.concatenate([cs[0:TX, :] * eb, cs[TX:, :] * eb], axis=0)
        send[pl.ds(b * SLOT + NX + 1, GX, stride=BLK), :] = dot(t12t[...], spread)


def store_table(lhs, n, table):
    turned = table.T
    hi = turned.astype(BF16)
    lhs[2 * n * NY : (2 * n + 1) * NY, :] = hi
    lhs[(2 * n + 1) * NY : (2 * n + 2) * NY, :] = (turned - hi.astype(F32)).astype(BF16)


def masks_of(cells):
    width = cells.shape[1]
    rowid = ((cells >> 7) & (NX - 1)) * NZ + (cells >> 10)
    each = iota((ROWS, width), 0).astype(F32).astype(BF16)
    hot = jnp.where(
        each == rowid.astype(F32).astype(BF16), jnp.array(1.0, BF16), jnp.array(0.0, BF16)
    )
    pick = iota((NY, width), 0) == (cells & (NY - 1))
    return hot, pick


def gather_all(lhs, count, cell, air):
    for n in range(9):
        for at in range(0, CAP, CHUNK):
            hot, pick = masks_of(cell[n : n + 1, at : at + CHUNK])
            got = jnp.dot(lhs[...], hot, preferred_element_type=F32)
            for f in range(count):
                a = 2 * f * NY
                both = got[a : a + NY] + got[a + NY : a + 2 * NY]
                air[f, n : n + 1, at : at + CHUNK] = jnp.sum(
                    jnp.where(pick, both, 0.0), axis=0, keepdims=True
                )


CHUNK = 512


def heat_kernel(fields, ylo_in, yhi_in, mid, mlo, mhi, clo, chi, after, stars, lhs, cell_out, state, done, zs):
    done[...] = jnp.zeros_like(done)
    lane = iota((NZ, NY), 1)
    ylo = ylo_in[0:NZ, :]
    yhi = yhi_in[0:NZ, :]
    vel = [velocity_rows(fields, x) for x in range(NX)]

    def side(msg, n):
        parts = []
        for g in range(4):
            k = n * 4 + g
            a, c = 40 + 8 * (k // 8), NY * (k % 8)
            parts.append(msg[a : a + 8, c : c + NY])
        return jnp.concatenate(parts, axis=0)

    for f in range(2):
        rows = [side(clo, f * 3 + i) for i in range(3)]
        rows += [field_row(fields, 3 + f, x) for x in range(NX)]
        rows += [side(chi, f * 3 + i) for i in range(3)]
        for x in range(NX):
            star = star_row(x, rows, ylo, yhi, 3 + f, vel[x], zs.at[f * NX + x], lane)
            at = (f * NX + x) * NZ
            stars[at : at + NZ, :] = star
        store_table(lhs, f, stars[f * ROWS : (f + 1) * ROWS, :])
    for r in range(3):
        for s in range(3):
            n = r * 3 + s
            if r == 1:
                block = block_of((mlo, mid, mhi)[s], (1, 0, 1)[s])
            else:
                block = block_of((clo, None, chi)[r], (0, 2, 1)[s])
            values, cell, count = block
            for a in range(10):
                state[a, n : n + 1, :] = values[a : a + 1]
            cell_out[n : n + 1, :] = cell.astype(jnp.int32)
            slot = iota((1, CAP), 1).astype(F32)
            state[10, n : n + 1, :] = jnp.where(slot < count, 1.0, 0.0)


def growth_kernel(lhs, cell, state, after, state_out, gain_out, done, air):
    done[...] = jnp.zeros_like(done)
    gather_all(lhs, 2, cell, air)
    live = state[10]
    radius = state[6]
    cubed = radius * radius * radius
    keeping = jnp.exp(-DT / (RELAX_TIME * radius * radius))
    saturation = air[1] * jnp.exp(-SATURATION_RATE * air[0]) - 1.0
    squared = radius * radius + GROWTH * (
        saturation - CURVATURE / radius + SOLUTE_EFFECT * state[8] / cubed
    )
    new_radius = jnp.sqrt(jnp.maximum(squared, RADIUS_FLOOR * RADIUS_FLOOR))
    gain_out[...] = live * state[7] * (new_radius * new_radius * new_radius - cubed)
    state_out[6] = new_radius * live
    state_out[7] = state[7] * live
    state_out[8] = state[8] * live
    state_out[9] = (state[9] + DT) * live
    for a in range(3):
        state_out[a] = state[a] * live
        state_out[3 + a] = state[3 + a] * (keeping * live)
    state_out[10] = (1.0 - keeping) * live


def scatter_kernel(stars, cell, gain, after, heat_next, moist_next, acc):
    acc[...] = jnp.zeros_like(acc)

    for n in range(9):
        for at in range(0, CAP, CHUNK):
            hot, pick = masks_of(cell[n : n + 1, at : at + CHUNK])
            g = gain[n : n + 1, at : at + CHUNK]
            hi = g.astype(BF16).astype(F32)
            z = jnp.concatenate(
                [
                    jnp.where(pick, hi, 0.0).astype(BF16),
                    jnp.where(pick, g - hi, 0.0).astype(BF16),
                ],
                axis=0,
            )
            acc[...] += lax.dot_general(
                hot, z, (((1,), (1,)), ((), ())), preferred_element_type=F32
            )
    for x in range(NX):
        a = x * NZ
        condensed = acc[a : a + NZ, 0:NY] + acc[a : a + NZ, NY:]
        heat_next[pl.ds(x, NZ, stride=NX), :] = stars[a : a + NZ, :] + HEAT_LOAD * condensed
        moist_next[pl.ds(x, NZ, stride=NX), :] = (
            stars[ROWS + a : ROWS + a + NZ, :] - MOIST_LOAD * condensed
        )


def final_kernel(
    recv, east_s, north_s, rise_s, zback, cell, state, east_next, north_next, up_next, drops_out, lhs, next_rows, air
):
    lane = iota((NZ, NY), 1)
    tiles = []
    for t in range(NX + 2):
        tiles.append(
            jnp.concatenate(
                [recv[pl.ds(b * SLOT + t, GX, stride=BLK), :] for b in range(2)], axis=0
            )
        )
    both = dot(zback[...], jnp.concatenate(tiles, axis=1))
    pres = [both[:NZ, t * NY : (t + 1) * NY] for t in range(NX + 2)]
    edge = pres[NX + 1]
    for x in range(NX):
        east = field_row(east_s, 0, x) - (pres[x + 1] - pres[x]) * ASPECT
        ahead = pltpu.roll(
            jnp.where(lane == 0, pltpu.roll(edge, (NY - x) % NY, 1), pres[x]), NY - 1, 1
        )
        north = field_row(north_s, 0, x) - (ahead - pres[x])
        rise = field_row(rise_s, 0, x) - both[NZ:, x * NY : (x + 1) * NY]
        for f, (val, ref) in enumerate(
            ((east, east_next), (north, north_next), (rise, up_next))
        ):
            ref[pl.ds(x, NZ, stride=NX), :] = val
            next_rows[f, x * NZ : (x + 1) * NZ, :] = val
    for f in range(3):
        store_table(lhs, f, next_rows[f])

    gather_all(lhs, 3, cell, air)
    mix = state[10]
    for a in range(3):
        speed = air[a] * mix + state[3 + a]
        offset = state[a] + DT * speed
        for r in range(3):
            drops_out[r, 3 + a] = speed[3 * r : 3 * r + 3]
            drops_out[r, a] = offset[3 * r : 3 * r + 3]
    for a in range(6, 10):
        for r in range(3):
            drops_out[r, a] = state[a, 3 * r : 3 * r + 3, :]


VM = pl.BlockSpec(memory_space=pltpu.VMEM)
SM = pl.BlockSpec(memory_space=pltpu.SMEM)
ANY = pl.BlockSpec(memory_space=pl.ANY)
HBM = pl.BlockSpec(memory_space=pltpu.HBM)


def sds(*shape, dtype=F32):
    return jax.ShapeDtypeStruct(shape, dtype)


TOKEN = sds(8, NY)


def call(kernel, name, us, out_shape, in_specs, scratch=(), mib=6, aliases=None):
    return pl.pallas_call(
        kernel,
        out_shape=out_shape,
        in_specs=in_specs,
        out_specs=tuple(VM for _ in out_shape),
        scratch_shapes=list(scratch),
        input_output_aliases=aliases or {},
        compiler_params=pltpu.CompilerParams(vmem_limit_bytes=mib * 1024 * 1024),
        cost_estimate=pl.CostEstimate(
            flops=int(us * 5e8), bytes_accessed=int(us * 2e6), transcendentals=0
        ),
        name=name,
    )


def ring(axis, shift):
    count = lax.axis_size(axis)
    return [(i, (i + shift) % count) for i in range(count)]


def per_device(u, v, w, h, q, droplets, cells, counts):
    tab = make_tables()
    u, v, w, h, q = (a.reshape(ROWS, NY) for a in (u, v, w, h, q))
    drops = droplets.transpose(0, 2, 1, 3)
    xlo, xhi, ylo, yhi, done = call(
        sides_kernel,
        "sides",
        2.0,
        (sds(9 * NZ, NY), sds(9 * NZ, NY), sds(9 * NZ, NY), sds(9 * NZ, NY), TOKEN),
        [HBM] * 5,
        [pltpu.VMEM((5 * ROWS, NY), F32), pltpu.SemaphoreType.DMA((5,))],
        60,
    )(u, v, w, h, q)
    xlo = lax.ppermute(xlo, "gx", ring("gx", 1))
    xhi = lax.ppermute(xhi, "gx", ring("gx", -1))
    ylo = lax.ppermute(ylo, "gy", ring("gy", 1))
    yhi = lax.ppermute(yhi, "gy", ring("gy", -1))
    up, down, mid, part, fields, tabs = call(
        pack_kernel,
        "pack",
        2.5,
        (
            sds(40, CAP), sds(40, CAP), sds(16, CAP), sds(80, CAP), sds(5 * ROWS, NY),
            sds(6 * TX + 16, NY),
        ),
        [HBM] * 6 + [VM, SM, HBM, ANY],
        [
            pltpu.VMEM((3, 10, 3, CAP), F32),
            pltpu.SemaphoreType.DMA((7,)),
        ],
        60,
    )(u, v, w, h, q, drops, cells, counts, tab["own"], done)
    mlo = lax.ppermute(up, "gy", ring("gy", 1))
    mhi = lax.ppermute(down, "gy", ring("gy", -1))
    east_s, north_s, rise_s, send, done = call(
        wind_kernel,
        "winds",
        3.0,
        (sds(ROWS, NY), sds(ROWS, NY), sds(ROWS, NY), sds(GX * BLK, NY), TOKEN),
        [VM] * 6,
        [pltpu.VMEM((3 * NX, NZ + 16, NY), F32)],
    )(fields, xlo, xhi, ylo, yhi, tab["ztab"])
    recv = lax.all_to_all(send.reshape(GX, BLK, NY), "gx", 0, 0, tiled=True)
    cup, cdown, done = call(
        relay_kernel, "relay", 1.0, (sds(64, CAP), sds(64, CAP), TOKEN), [VM] * 3 + [ANY]
    )(part, mlo, mhi, done)
    clo = lax.ppermute(cup, "gx", ring("gx", 1))
    chi = lax.ppermute(cdown, "gx", ring("gx", -1))
    msg, keep, kink, done = call(
        scan_kernel,
        "scan",
        2.0,
        (sds(8 * GY, NY), sds(2 * TX, NY), sds(8, NY), TOKEN),
        [VM] * 5 + [ANY],
    )(
        recv.reshape(GX * BLK, NY), tab["wmain"], tab["t12"], tab["cs"], tabs, done
    )
    got = lax.all_to_all(msg.reshape(GY, 8, NY), "gy", 0, 0, tiled=True)
    stars_hq, lhs, cell_in, state, done = call(
        heat_kernel,
        "heat",
        3.0,
        (
            sds(2 * ROWS, NY), sds(4 * NY, ROWS, dtype=BF16),
            sds(9, CAP, dtype=jnp.int32), sds(11, 9, CAP), TOKEN,
        ),
        [VM] * 8 + [ANY],
        [pltpu.VMEM((2 * NX, NZ + 16, NY), F32)],
    )(fields, ylo, yhi, mid, mlo, mhi, clo, chi, done)
    state, gain, done = call(
        growth_kernel,
        "growth",
        5.0,
        (sds(11, 9, CAP), sds(9, CAP), TOKEN),
        [VM] * 3 + [ANY],
        [pltpu.VMEM((2, 9, CAP), F32)],
    )(lhs, cell_in, state, done)
    send, done = call(
        solve_kernel, "solve", 2.0, (sds(GX * BLK, NY), TOKEN), [VM] * 7 + [ANY]
    )(
        got.reshape(8 * GY, NY), keep, kink, tab["wback"], tab["t12t"], tab["cs"], tabs,
        done,
    )
    recv = lax.all_to_all(send.reshape(GX, BLK, NY), "gx", 0, 0, tiled=True)
    heat_next, moist_next = call(
        scatter_kernel,
        "scatter",
        4.0,
        (sds(ROWS, NY), sds(ROWS, NY)),
        [VM] * 3 + [ANY],
        [pltpu.VMEM((ROWS, 2 * NY), F32)],
    )(stars_hq, cell_in, gain, done)
    east_next, north_next, up_next, drops_out = call(
        final_kernel,
        "final",
        8.0,
        (sds(ROWS, NY), sds(ROWS, NY), sds(ROWS, NY), sds(3, 10, 3, CAP)),
        [VM] * 7,
        [
            pltpu.VMEM((6 * NY, ROWS), BF16),
            pltpu.VMEM((3, ROWS, NY), F32),
            pltpu.VMEM((3, 9, CAP), F32),
        ],
        aliases={1: 0, 2: 1, 3: 2},
    )(recv.reshape(GX * BLK, NY), east_s, north_s, rise_s, tab["zback"], cell_in, state)
    out = (
        a.reshape(NZ, NX, NY) for a in (east_next, north_next, up_next, heat_next, moist_next)
    )
    return (*out, drops_out.transpose(0, 2, 1, 3))


def solution(mesh):
    grid = P(None, "gx", "gy")
    blocks = P("gx", "gy", None, None)
    return jax.shard_map(
        per_device,
        mesh=mesh,
        in_specs=(grid,) * 5 + (blocks, P("gx", "gy", None), P("gx", "gy")),
        out_specs=(grid,) * 5 + (blocks,),
        check_vma=False,
    )
```

```python
import math

import jax
import jax.numpy as jnp
import numpy as np
from jax import lax
from jax.experimental import pallas as pl
from jax.experimental.pallas import tpu as pltpu
from jax.sharding import PartitionSpec as P

DT = 0.2
RELAX_TIME = 0.2
GROWTH = 0.5
CURVATURE = 0.1
SOLUTE_EFFECT = 0.05
RADIUS_FLOOR = 0.3
SATURATION_RATE = 0.1
MOIST_LOAD = 0.5
HEAT_LOAD = 1.25
ASPECT = 0.0625
HIGHEST = lax.Precision.HIGHEST

NZ = 32
NX = 8
NY = 128
GX = 16
GY = 16
TX = NX * GX
TY = NY * GY
CAP = 1024
ROWS = NZ * NX
SLOT = 12
BLK = 2 * SLOT
F32 = jnp.float32
BF16 = jnp.bfloat16


def make_tables():
    m = np.arange(NZ)
    ztab = np.cos(np.pi * m[:, None] * (2 * m[None, :] + 1) / (2 * NZ)) * np.where(
        m[:, None] == 0, math.sqrt(1.0 / NZ), math.sqrt(2.0 / NZ)
    )
    zdiff = np.zeros((NZ, NZ))
    zdiff[:-1] = (ztab.T[1:] - ztab.T[:-1]) * ASPECT
    zback = np.concatenate([ztab.T, zdiff], axis=0)
    p = np.arange(TX)

    def cas(a):
        return np.cos(a) + np.sin(a)

    w = 2 * np.pi / TX
    har = cas(w * (p[:, None] * p[None, :] % TX)) / math.sqrt(TX)
    wmain = np.zeros((2, TX, GX, 2, SLOT))
    for X in range(GX):
        for t in range(NX + 1):
            for b in range(2):
                wmain[b, :, X, b, t] = har[:, (NX * X + t) % TX]
    wmain = wmain.reshape(2 * TX, GX * BLK)
    X = np.arange(GX)
    t12 = np.concatenate(
        [cas(w * p[:, None] * NX * X[None, :]), cas(-w * p[:, None] * NX * X[None, :])], axis=0
    ) / math.sqrt(TX)
    lane = np.arange(NY)
    cosx = np.where(lane[None, :] < NX, np.cos(w * p[:, None] * lane[None, :]), 0.0)
    sinx = np.where(lane[None, :] < NX, np.sin(w * p[:, None] * lane[None, :]), 0.0)
    cs = np.concatenate([cosx, sinx], axis=0)
    lam = (
        (2 - 2 * np.cos(np.pi * m[:, None] / NZ)) + (2 - 2 * np.cos(w * p[None, :]))
    ) * ASPECT
    zero = lam <= 0
    lam = np.where(zero, 0.5, lam)
    lnr = -2.0 * np.arcsinh(np.sqrt(lam) / 2.0)
    coef = np.where(zero, 0.0, -1.0 / (2.0 * np.sinh(-lnr)))
    lnr = lnr.reshape(2, GX, TX).transpose(1, 0, 2).reshape(GX, 2 * TX)
    coef = coef.reshape(2, GX, TX).transpose(1, 0, 2).reshape(GX, 2 * TX)
    misc = np.zeros((GX, 2 * TX, NY))
    for k in range(8):
        misc[:, :, k] = np.exp(lnr * (1 << k))
    misc[:, :, 8] = coef
    rowtab = np.zeros((GX, 8, 2 * TX))
    rowtab[:, 0] = NY * lnr
    rowtab[:, 1] = 1.0 / (1.0 - np.exp(lnr * TY))
    misc[:, :, 9] = lnr
    own = np.concatenate([misc, rowtab[:, :, :NY], rowtab[:, :, NY:]], axis=1)

    def f(a):
        return jnp.asarray(np.asarray(a, np.float32))

    return dict(
        ztab=f(ztab),
        zback=f(zback),
        wmain=f(wmain),
        wback=f(wmain.T),
        t12=f(t12),
        t12t=f(t12.T),
        cs=f(cs),
        own=f(own),
    )


def iota(shape, dim):
    return lax.broadcasted_iota(jnp.int32, shape, dim)


def dot(a, b):
    return jnp.dot(a, b, precision=HIGHEST, preferred_element_type=F32)


def field_row(fields, f, x):
    return fields[pl.ds(f * ROWS + x, NZ, stride=NX), :]


def pair_of(f0, lo, hi):
    d1, d2, d3 = (h - l for l, h in zip(lo, hi))
    s1, s2, s3 = (h + l for l, h in zip(lo, hi))
    return (45.0 * d1 - 9.0 * d2 + d3, 20.0 * f0 - 15.0 * s1 + 6.0 * s2 - s3)


def star_row(x, rows, ylo, yhi, slot, velocity, zs, lane):
    f0 = rows[x + 3]
    zs[8 : 8 + NZ, :] = f0
    zs[0:8, :] = jnp.broadcast_to(f0[0:1], (8, NY))
    zs[8 + NZ : 16 + NZ, :] = jnp.broadcast_to(f0[NZ - 1 : NZ], (8, NY))
    au, bu, av, bv, aw, bw = velocity
    a, b = pair_of(
        f0, [rows[x + 3 - k] for k in (1, 2, 3)], [rows[x + 3 + k] for k in (1, 2, 3)]
    )
    total = au * a + bu * b
    where_lo = 16 * x + 3 * slot
    halo = jnp.where(
        lane >= 64,
        pltpu.roll(ylo, (125 - where_lo) % NY, 1),
        pltpu.roll(yhi, (NY - where_lo) % NY, 1),
    )
    lo = [pltpu.roll(jnp.where(lane >= NY - k, halo, f0), k, 1) for k in (1, 2, 3)]
    hi = [pltpu.roll(jnp.where(lane < k, halo, f0), NY - k, 1) for k in (1, 2, 3)]
    a, b = pair_of(f0, lo, hi)
    total = total + (av * a + bv * b)
    a, b = pair_of(
        f0,
        [zs[8 - k : 8 - k + NZ, :] for k in (1, 2, 3)],
        [zs[8 + k : 8 + k + NZ, :] for k in (1, 2, 3)],
    )
    return f0 - (total + (aw * a + bw * b))


def velocity_rows(fields, x):
    out = []
    for f in range(3):
        a = field_row(fields, f, x) * (DT / 60.0)
        out += [a, jnp.abs(a)]
    return out


def sides_kernel(u, v, w, h, q, xlo, xhi, ylo, yhi, fields, done, sems):
    done[...] = jnp.zeros_like(done)
    copies = [
        pltpu.make_async_copy(ref, fields.at[pl.ds(f * ROWS, ROWS)], sems.at[f])
        for f, ref in enumerate((u, v, w, h, q))
    ]
    for copy in copies:
        copy.start()
    for copy in copies:
        copy.wait()
    for f in range(5):
        for i in range(3):
            n = f * 3 + i
            xlo[n * NZ : (n + 1) * NZ, :] = field_row(fields, f, 5 + i)
            xhi[n * NZ : (n + 1) * NZ, :] = field_row(fields, f, i)
    lane = iota((NZ, NY), 1)
    tlo = jnp.zeros((NZ, NY), F32)
    thi = jnp.zeros((NZ, NY), F32)
    for x in range(NX):
        for f in range(5):
            at = 16 * x + 3 * f
            row = field_row(fields, f, x)
            mask = (lane >= at) & (lane < at + 3)
            tlo = jnp.where(mask, pltpu.roll(row, (at - 125) % NY, 1), tlo)
            thi = jnp.where(mask, pltpu.roll(row, at, 1), thi)
    ylo[0:NZ, :] = tlo
    yhi[0:NZ, :] = thi
    ylo[NZ:, :] = jnp.zeros((8 * NZ, NY), F32)
    yhi[NZ:, :] = jnp.zeros((8 * NZ, NY), F32)


def pack_kernel(
    drops_in, cells, counts, own, after, up, down, mid, part, tabs, drops, sems
):
    copies = [
        pltpu.make_async_copy(drops_in, drops, sems.at[0]),
        pltpu.make_async_copy(own.at[lax.axis_index("gx")], tabs, sems.at[1]),
    ]
    for copy in copies:
        copy.start()
    copies[0].wait()
    for out, at, r, s in (
        [(up, r * SLOT, r, 2) for r in range(3)]
        + [(down, r * SLOT, r, 0) for r in range(3)]
        + [(mid, 0, 1, 1), (part, 0, 2, 1), (part, 16, 0, 1)]
    ):
        for a in range(10):
            out[at + a : at + a + 1, :] = drops[r, a, s : s + 1, :]
        out[at + 10 : at + 11, :] = cells[r, s : s + 1, :].astype(F32)
        out[at + 11 : at + 12, :] = jnp.full((1, CAP), counts[r, s], jnp.int32).astype(F32)
    for out, at, rows in ((up, 36, 4), (down, 36, 4), (mid, 12, 4), (part, 12, 4), (part, 28, 4)):
        out[at : at + rows, :] = jnp.zeros((rows, CAP), F32)
    copies[1].wait()


def hop_kernel(up, down, after, up_out, down_out, done):
    done[...] = jnp.zeros_like(done)


def block_of(msg, n):
    return (
        msg[n * SLOT : n * SLOT + 10, :],
        msg[n * SLOT + 10 : n * SLOT + 11, :],
        msg[n * SLOT + 11 : n * SLOT + 12, :],
    )


def relay_kernel(part, mlo, mhi, after, up, down, done):
    done[...] = jnp.zeros_like(done)
    for n, (out, r) in enumerate(((up, 2), (down, 0))):
        out[0:12, :] = mlo[r * SLOT : (r + 1) * SLOT, :]
        out[12:24, :] = mhi[r * SLOT : (r + 1) * SLOT, :]
        out[24:40, :] = part[n * 16 : (n + 1) * 16, :]


def wind_kernel(fields, xlo, xhi, ylo_in, yhi_in, ztab, east_s, north_s, rise_s, send, done, zs):
    done[...] = jnp.zeros_like(done)
    lane = iota((NZ, NY), 1)
    level = iota((NZ, NY), 0)
    ylo = ylo_in[0:NZ, :]
    yhi = yhi_in[0:NZ, :]
    vel = [velocity_rows(fields, x) for x in range(NX)]
    for f in range(3):
        rows = [xlo[(f * 3 + i) * NZ : (f * 3 + i + 1) * NZ, :] for i in range(3)]
        rows += [field_row(fields, f, x) for x in range(NX)]
        rows += [xhi[(f * 3 + i) * NZ : (f * 3 + i + 1) * NZ, :] for i in range(3)]
        for x in range(NX):
            star = star_row(x, rows, ylo, yhi, f, vel[x], zs.at[f * NX + x], lane)
            if f == 2:
                star = jnp.where(level == NZ - 1, 0.0, star)
            (east_s, north_s, rise_s)[f][pl.ds(x, NZ, stride=NX), :] = star
    tiles = []
    ext = jnp.zeros((NZ, NY), F32)
    for x in range(NX):
        east = field_row(east_s, 0, x)
        north = field_row(north_s, 0, x)
        rise = field_row(rise_s, 0, x)
        d = east + north + rise
        if x > 0:
            d = d - field_row(east_s, 0, x - 1)
        d = d - jnp.where(lane == 0, 0.0, pltpu.roll(north, 1, 1))
        d = d - jnp.where(level == 0, 0.0, pltpu.roll(rise, 1, 0))
        tiles.append(d)
        ext = jnp.where(lane == x, -pltpu.roll(north, (x + 1) % NY, 1), ext)
    tiles.append(-field_row(east_s, 0, NX - 1))
    tiles.append(ext)
    hat = dot(ztab[...], jnp.concatenate(tiles, axis=1))
    zeros = jnp.zeros((GX, NY), F32)
    for b in range(2):
        for t in range(SLOT):
            if t < NX + 2:
                val = hat[b * GX : (b + 1) * GX, t * NY : (t + 1) * NY]
            else:
                val = zeros
            send[pl.ds(b * SLOT + t, GX, stride=BLK), :] = val


def own_tables(tabs):
    n = 2 * TX
    return tabs.at[0:n], tabs.at[n : n + 16]


def scan_kernel(recv, wmain, t12, cs, tabs, after, msg, keep, kink, done):
    done[...] = jnp.zeros_like(done)
    misc, rowtab = own_tables(tabs)
    lane = iota((2 * TX, NY), 1)
    d = dot(wmain[...], recv[...])
    ends = []
    for b in range(2):
        e16 = recv[pl.ds(b * SLOT + NX + 1, GX, stride=BLK), :]
        prod = dot(t12[...], e16) * cs[...]
        ends.append(jnp.sum(prod[:TX] + prod[TX:], axis=1, keepdims=True))
    e = jnp.concatenate(ends, axis=0)
    fwd = d
    bwd = d
    for k in range(7):
        s = 1 << k
        a = jnp.broadcast_to(misc[:, k : k + 1], (2 * TX, NY))
        fwd = fwd + jnp.where(lane >= s, a * pltpu.roll(fwd, s, 1), 0.0)
        bwd = bwd + jnp.where(lane < NY - s, a * pltpu.roll(bwd, NY - s, 1), 0.0)
    r1 = misc[:, 0:1]
    r128 = misc[:, 7:8]
    out_right = r1 * fwd[:, NY - 1 : NY] + e
    out_left = bwd[:, 0:1] + r128 * e
    from_end = float(NY) - lane.astype(F32)
    keep[...] = fwd + bwd - d + jnp.exp(from_end * misc[:, 9:10]) * e
    lane1 = lane[:TX]
    table = jnp.zeros((TX, NY), F32)
    for b in range(2):
        table = jnp.where(lane1 == b, out_right[b * TX : (b + 1) * TX], table)
        table = jnp.where(lane1 == 2 + b, out_left[b * TX : (b + 1) * TX], table)
    d8 = d[0:8]
    e8 = e[0:8]
    lane8 = iota((8, NY), 1)
    lanef = lane8.astype(F32)
    s0 = jnp.sum(d8, axis=1, keepdims=True) + e8
    s1 = jnp.sum(d8 * lanef, axis=1, keepdims=True) + float(NY) * e8
    top = jnp.where(lane8 == 4, s0, jnp.where(lane8 == 5, s1, table[0:8]))
    table = jnp.concatenate([top, table[8:]], axis=0)
    turned = table.T[0:8]
    for y in range(GY):
        msg[y * 8 : (y + 1) * 8, :] = turned
    apart = jnp.abs(iota((NY, NY), 0) - iota((NY, NY), 1)).astype(F32)
    kink[...] = dot(d8, apart) + e8 * (float(NY) - lanef)


def solve_kernel(got, keep, kink, wback, t12t, cs, tabs, after, send, done):
    done[...] = jnp.zeros_like(done)
    misc, rowtab = own_tables(tabs)
    here = lax.axis_index("gy")
    first = (lax.axis_index("gx") == 0).astype(F32)
    who = iota((GY, 2 * TX), 0)
    def rows(k):
        return jnp.concatenate([got[y * 8 + k : y * 8 + k + 1, :] for y in range(GY)], axis=0)

    all_right = jnp.concatenate([rows(0), rows(1)], axis=1)
    all_left = jnp.concatenate([rows(2), rows(3)], axis=1)
    s0 = rows(4)[:, 0:1]
    s1 = rows(5)[:, 0:1]
    lnr = jnp.concatenate([rowtab[0:1, :], rowtab[8:9, :]], axis=1)
    inv = jnp.concatenate([rowtab[1:2, :], rowtab[9:10, :]], axis=1)
    after = ((here - who - 1) & (GY - 1)).astype(F32)
    before = ((who - here - 1) & (GY - 1)).astype(F32)
    in_left = jnp.sum(jnp.exp(after * lnr) * all_right, axis=0, keepdims=True) * inv
    in_right = jnp.sum(jnp.exp(before * lnr) * all_left, axis=0, keepdims=True) * inv
    own_right = jnp.sum(jnp.where(who == here, all_right, 0.0), axis=0, keepdims=True)
    row = iota((8, 2 * TX), 0)
    turned = jnp.where(row == 0, in_left, jnp.where(row == 1, in_right, own_right)).T
    in_left = turned[:, 0:1]
    in_right = turned[:, 1:2]
    coef = misc[:, 8:9]
    lnc = jnp.broadcast_to(misc[:, 9:10], (2 * TX, NY))
    at = iota((2 * TX, NY), 1).astype(F32)
    pres = coef * (
        keep[...] + jnp.exp(at * lnc) * in_left + jnp.exp((float(NY) - at) * lnc) * in_right
    )
    edge = coef * (turned[:, 2:3] + misc[:, 7:8] * in_left + in_right)
    who1 = iota((GY, 1), 0)
    far = (NY * ((here - who1) & (GY - 1))).astype(F32)
    mine = who1 == here
    sum0 = jnp.sum(s0, axis=0, keepdims=True)
    own0 = jnp.sum(jnp.where(mine, s0, 0.0), axis=0, keepdims=True)
    own1 = jnp.sum(jnp.where(mine, s1, 0.0), axis=0, keepdims=True)
    lin = 0.5 * (sum0 - own0) + jnp.sum(s1 - far * s0, axis=0, keepdims=True) * (1.0 / TY)
    quad = sum0 * (0.5 / TY)
    lanef = iota((8, NY), 1).astype(F32)
    top = 0.5 * kink[...] + lanef * (lin - lanef * quad)
    edge0 = 0.5 * (float(NY) * own0 - own1) + float(NY) * (lin - float(NY) * quad)
    row8 = iota((8, NY), 0)
    top = pres[0:8] + jnp.where(row8 == 0, first * top, 0.0)
    pres = jnp.concatenate([top, pres[8:]], axis=0)
    row1 = iota((2 * TX, 1), 0)
    edge = edge + jnp.where(row1 == 0, first * edge0, 0.0)
    send[...] = dot(wback[...], pres)
    for b in range(2):
        eb = edge[b * TX : (b + 1) * TX]
        spread = jnp.concatenate([cs[0:TX, :] * eb, cs[TX:, :] * eb], axis=0)
        send[pl.ds(b * SLOT + NX + 1, GX, stride=BLK), :] = dot(t12t[...], spread)


def store_table(lhs, n, table):
    turned = table.T
    hi = turned.astype(BF16)
    lhs[2 * n * NY : (2 * n + 1) * NY, :] = hi
    lhs[(2 * n + 1) * NY : (2 * n + 2) * NY, :] = (turned - hi.astype(F32)).astype(BF16)


def masks_of(cells):
    width = cells.shape[1]
    rowid = ((cells >> 7) & (NX - 1)) * NZ + (cells >> 10)
    each = iota((ROWS, width), 0).astype(F32).astype(BF16)
    hot = jnp.where(
        each == rowid.astype(F32).astype(BF16), jnp.array(1.0, BF16), jnp.array(0.0, BF16)
    )
    pick = iota((NY, width), 0) == (cells & (NY - 1))
    return hot, pick


def gather_all(lhs, count, cell, air):
    for n in range(9):
        for at in range(0, CAP, CHUNK):
            hot, pick = masks_of(cell[n : n + 1, at : at + CHUNK])
            got = jnp.dot(lhs[...], hot, preferred_element_type=F32)
            for f in range(count):
                a = 2 * f * NY
                both = got[a : a + NY] + got[a + NY : a + 2 * NY]
                air[f, n : n + 1, at : at + CHUNK] = jnp.sum(
                    jnp.where(pick, both, 0.0), axis=0, keepdims=True
                )


CHUNK = 512


def heat_kernel(fields, ylo_in, yhi_in, xlo, xhi, after, stars, lhs, done, zs):
    done[...] = jnp.zeros_like(done)
    lane = iota((NZ, NY), 1)
    ylo = ylo_in[0:NZ, :]
    yhi = yhi_in[0:NZ, :]
    vel = [velocity_rows(fields, x) for x in range(NX)]

    for f in range(2):
        rows = [xlo[(f * 3 + i + 9) * NZ : (f * 3 + i + 10) * NZ, :] for i in range(3)]
        rows += [field_row(fields, 3 + f, x) for x in range(NX)]
        rows += [xhi[(f * 3 + i + 9) * NZ : (f * 3 + i + 10) * NZ, :] for i in range(3)]
        for x in range(NX):
            star = star_row(x, rows, ylo, yhi, 3 + f, vel[x], zs.at[f * NX + x], lane)
            at = (f * NX + x) * NZ
            stars[at : at + NZ, :] = star
        store_table(lhs, f, stars[f * ROWS : (f + 1) * ROWS, :])


def unpack_kernel(mid, mlo, mhi, clo, chi, after, cell_out, state):
    for r in range(3):
        for s in range(3):
            n = r * 3 + s
            if r == 1:
                block = block_of((mlo, mid, mhi)[s], (1, 0, 1)[s])
            else:
                block = block_of((clo, None, chi)[r], (0, 2, 1)[s])
            values, cell, count = block
            for a in range(10):
                state[a, n : n + 1, :] = values[a : a + 1]
            cell_out[n : n + 1, :] = cell.astype(jnp.int32)
            slot = iota((1, CAP), 1).astype(F32)
            state[10, n : n + 1, :] = jnp.where(slot < count, 1.0, 0.0)


def growth_kernel(lhs, cell, state, state_out, gain, air):
    gather_all(lhs, 2, cell, air)
    live = state[10]
    radius = state[6]
    cubed = radius * radius * radius
    keeping = jnp.exp(-DT / (RELAX_TIME * radius * radius))
    saturation = air[1] * jnp.exp(-SATURATION_RATE * air[0]) - 1.0
    squared = radius * radius + GROWTH * (
        saturation - CURVATURE / radius + SOLUTE_EFFECT * state[8] / cubed
    )
    new_radius = jnp.sqrt(jnp.maximum(squared, RADIUS_FLOOR * RADIUS_FLOOR))
    gain[...] = live * state[7] * (new_radius * new_radius * new_radius - cubed)
    state_out[6] = new_radius * live
    state_out[7] = state[7] * live
    state_out[8] = state[8] * live
    state_out[9] = (state[9] + DT) * live
    for a in range(3):
        state_out[a] = state[a] * live
        state_out[3 + a] = state[3 + a] * (keeping * live)
    state_out[10] = (1.0 - keeping) * live


def scatter_kernel(stars, cell, gain, heat_next, moist_next, acc):
    acc[...] = jnp.zeros_like(acc)

    for n in range(9):
        for at in range(0, CAP, CHUNK):
            hot, pick = masks_of(cell[n : n + 1, at : at + CHUNK])
            g = gain[n : n + 1, at : at + CHUNK]
            hi = g.astype(BF16).astype(F32)
            z = jnp.concatenate(
                [
                    jnp.where(pick, hi, 0.0).astype(BF16),
                    jnp.where(pick, g - hi, 0.0).astype(BF16),
                ],
                axis=0,
            )
            acc[...] += lax.dot_general(
                hot, z, (((1,), (1,)), ((), ())), preferred_element_type=F32
            )
    for x in range(NX):
        a = x * NZ
        condensed = acc[a : a + NZ, 0:NY] + acc[a : a + NZ, NY:]
        heat_next[pl.ds(x, NZ, stride=NX), :] = stars[a : a + NZ, :] + HEAT_LOAD * condensed
        moist_next[pl.ds(x, NZ, stride=NX), :] = (
            stars[ROWS + a : ROWS + a + NZ, :] - MOIST_LOAD * condensed
        )


def final_kernel(
    recv, east_s, north_s, rise_s, zback, cell, state, east_next, north_next, up_next, drops_out, lhs, next_rows, air
):
    lane = iota((NZ, NY), 1)
    tiles = []
    for t in range(NX + 2):
        tiles.append(
            jnp.concatenate(
                [recv[pl.ds(b * SLOT + t, GX, stride=BLK), :] for b in range(2)], axis=0
            )
        )
    both = dot(zback[...], jnp.concatenate(tiles, axis=1))
    pres = [both[:NZ, t * NY : (t + 1) * NY] for t in range(NX + 2)]
    edge = pres[NX + 1]
    for x in range(NX):
        east = field_row(east_s, 0, x) - (pres[x + 1] - pres[x]) * ASPECT
        ahead = pltpu.roll(
            jnp.where(lane == 0, pltpu.roll(edge, (NY - x) % NY, 1), pres[x]), NY - 1, 1
        )
        north = field_row(north_s, 0, x) - (ahead - pres[x])
        rise = field_row(rise_s, 0, x) - both[NZ:, x * NY : (x + 1) * NY]
        for f, (val, ref) in enumerate(
            ((east, east_next), (north, north_next), (rise, up_next))
        ):
            ref[pl.ds(x, NZ, stride=NX), :] = val
            next_rows[f, x * NZ : (x + 1) * NZ, :] = val
    for f in range(3):
        store_table(lhs, f, next_rows[f])

    gather_all(lhs, 3, cell, air)
    mix = state[10]
    for a in range(3):
        speed = air[a] * mix + state[3 + a]
        offset = state[a] + DT * speed
        for r in range(3):
            drops_out[r, 3 + a] = speed[3 * r : 3 * r + 3]
            drops_out[r, a] = offset[3 * r : 3 * r + 3]
    for a in range(6, 10):
        for r in range(3):
            drops_out[r, a] = state[a, 3 * r : 3 * r + 3, :]


VM = pl.BlockSpec(memory_space=pltpu.VMEM)
SM = pl.BlockSpec(memory_space=pltpu.SMEM)
ANY = pl.BlockSpec(memory_space=pl.ANY)
HBM = pl.BlockSpec(memory_space=pltpu.HBM)


def sds(*shape, dtype=F32):
    return jax.ShapeDtypeStruct(shape, dtype)


TOKEN = sds(8, NY)


def call(kernel, name, us, out_shape, in_specs, scratch=(), mib=6, aliases=None, outs=None):
    return pl.pallas_call(
        kernel,
        out_shape=out_shape,
        in_specs=in_specs,
        out_specs=tuple(outs or [VM] * len(out_shape)),
        scratch_shapes=list(scratch),
        input_output_aliases=aliases or {},
        compiler_params=pltpu.CompilerParams(vmem_limit_bytes=mib * 1024 * 1024),
        cost_estimate=pl.CostEstimate(
            flops=int(us * 5e8), bytes_accessed=int(us * 2e6), transcendentals=0
        ),
        name=name,
    )


def ring(axis, shift):
    count = lax.axis_size(axis)
    return [(i, (i + shift) % count) for i in range(count)]


def per_device(u, v, w, h, q, droplets, cells, counts):
    tab = make_tables()
    u, v, w, h, q = (a.reshape(ROWS, NY) for a in (u, v, w, h, q))
    drops = droplets.transpose(0, 2, 1, 3)
    xlo, xhi, ylo, yhi, fields, done = call(
        sides_kernel,
        "sides",
        2.0,
        (
            sds(15 * NZ, NY), sds(15 * NZ, NY), sds(9 * NZ, NY), sds(9 * NZ, NY),
            sds(5 * ROWS, NY), TOKEN,
        ),
        [HBM] * 5,
        [pltpu.SemaphoreType.DMA((5,))],
        60,
    )(u, v, w, h, q)
    xlo = lax.ppermute(xlo, "gx", ring("gx", 1))
    xhi = lax.ppermute(xhi, "gx", ring("gx", -1))
    ylo = lax.ppermute(ylo, "gy", ring("gy", 1))
    yhi = lax.ppermute(yhi, "gy", ring("gy", -1))
    up, down, mid, part, tabs = call(
        pack_kernel,
        "pack",
        2.5,
        (sds(40, CAP), sds(40, CAP), sds(16, CAP), sds(32, CAP), sds(2 * TX + 16, NY)),
        [HBM, VM, SM, HBM, ANY],
        [pltpu.VMEM((3, 10, 3, CAP), F32), pltpu.SemaphoreType.DMA((2,))],
        60,
    )(drops, cells, counts, tab["own"], done)
    east_s, north_s, rise_s, send, done = call(
        wind_kernel,
        "winds",
        3.0,
        (sds(ROWS, NY), sds(ROWS, NY), sds(ROWS, NY), sds(GX * BLK, NY), TOKEN),
        [VM] * 6,
        [pltpu.VMEM((3 * NX, NZ + 16, NY), F32)],
    )(fields, xlo, xhi, ylo, yhi, tab["ztab"])
    recv = lax.all_to_all(send.reshape(GX, BLK, NY), "gx", 0, 0, tiled=True)
    up, down, done = call(
        hop_kernel,
        "hop",
        0.5,
        (sds(40, CAP), sds(40, CAP), TOKEN),
        [ANY] * 3,
        aliases={0: 0, 1: 1},
        outs=[ANY, ANY, VM],
    )(up, down, done)
    mlo = lax.ppermute(up, "gy", ring("gy", 1))
    mhi = lax.ppermute(down, "gy", ring("gy", -1))
    msg, keep, kink, done = call(
        scan_kernel,
        "scan",
        2.0,
        (sds(8 * GY, NY), sds(2 * TX, NY), sds(8, NY), TOKEN),
        [VM] * 5 + [ANY],
    )(
        recv.reshape(GX * BLK, NY), tab["wmain"], tab["t12"], tab["cs"], tabs, done
    )
    got = lax.all_to_all(msg.reshape(GY, 8, NY), "gy", 0, 0, tiled=True)
    stars_hq, lhs, done = call(
        heat_kernel,
        "heat",
        4.0,
        (sds(2 * ROWS, NY), sds(4 * NY, ROWS, dtype=BF16), TOKEN),
        [VM] * 5 + [ANY],
        [pltpu.VMEM((2 * NX, NZ + 16, NY), F32)],
    )(fields, ylo, yhi, xlo, xhi, done)
    cup, cdown, done = call(
        relay_kernel, "relay", 1.0, (sds(40, CAP), sds(40, CAP), TOKEN), [VM] * 3 + [ANY]
    )(part, mlo, mhi, done)
    clo = lax.ppermute(cup, "gx", ring("gx", 1))
    chi = lax.ppermute(cdown, "gx", ring("gx", -1))
    send, done = call(
        solve_kernel, "solve", 2.0, (sds(GX * BLK, NY), TOKEN), [VM] * 7 + [ANY]
    )(
        got.reshape(8 * GY, NY), keep, kink, tab["wback"], tab["t12t"], tab["cs"], tabs,
        done,
    )
    recv = lax.all_to_all(send.reshape(GX, BLK, NY), "gx", 0, 0, tiled=True)
    cell_in, state = call(
        unpack_kernel,
        "unpack",
        1.0,
        (sds(9, CAP, dtype=jnp.int32), sds(11, 9, CAP)),
        [VM] * 5 + [ANY],
    )(mid, mlo, mhi, clo, chi, done)
    state, gain = call(
        growth_kernel,
        "growth",
        5.0,
        (sds(11, 9, CAP), sds(9, CAP)),
        [VM] * 3,
        [pltpu.VMEM((2, 9, CAP), F32)],
    )(lhs, cell_in, state)
    heat_next, moist_next = call(
        scatter_kernel,
        "scatter",
        4.0,
        (sds(ROWS, NY), sds(ROWS, NY)),
        [VM] * 3,
        [pltpu.VMEM((ROWS, 2 * NY), F32)],
    )(stars_hq, cell_in, gain)
    east_next, north_next, up_next, drops_out = call(
        final_kernel,
        "final",
        8.0,
        (sds(ROWS, NY), sds(ROWS, NY), sds(ROWS, NY), sds(3, 10, 3, CAP)),
        [VM] * 7,
        [
            pltpu.VMEM((6 * NY, ROWS), BF16),
            pltpu.VMEM((3, ROWS, NY), F32),
            pltpu.VMEM((3, 9, CAP), F32),
        ],
        aliases={1: 0, 2: 1, 3: 2},
    )(recv.reshape(GX * BLK, NY), east_s, north_s, rise_s, tab["zback"], cell_in, state)
    out = (
        a.reshape(NZ, NX, NY) for a in (east_next, north_next, up_next, heat_next, moist_next)
    )
    return (*out, drops_out.transpose(0, 2, 1, 3))


def solution(mesh):
    grid = P(None, "gx", "gy")
    blocks = P("gx", "gy", None, None)
    return jax.shard_map(
        per_device,
        mesh=mesh,
        in_specs=(grid,) * 5 + (blocks, P("gx", "gy", None), P("gx", "gy")),
        out_specs=(grid,) * 5 + (blocks,),
        check_vma=False,
    )
```

```python
import math

import jax
import jax.numpy as jnp
import numpy as np
from jax import lax
from jax.experimental import pallas as pl
from jax.experimental.pallas import tpu as pltpu
from jax.sharding import PartitionSpec as P

DT = 0.2
RELAX_TIME = 0.2
GROWTH = 0.5
CURVATURE = 0.1
SOLUTE_EFFECT = 0.05
RADIUS_FLOOR = 0.3
SATURATION_RATE = 0.1
MOIST_LOAD = 0.5
HEAT_LOAD = 1.25
ASPECT = 0.0625
HIGHEST = lax.Precision.HIGHEST

NZ = 32
NX = 8
NY = 128
GX = 16
GY = 16
TX = NX * GX
TY = NY * GY
CAP = 1024
ROWS = NZ * NX
SLOT = 12
BLK = 2 * SLOT
F32 = jnp.float32
BF16 = jnp.bfloat16


def make_tables():
    m = np.arange(NZ)
    ztab = np.cos(np.pi * m[:, None] * (2 * m[None, :] + 1) / (2 * NZ)) * np.where(
        m[:, None] == 0, math.sqrt(1.0 / NZ), math.sqrt(2.0 / NZ)
    )
    zdiff = np.zeros((NZ, NZ))
    zdiff[:-1] = (ztab.T[1:] - ztab.T[:-1]) * ASPECT
    zback = np.concatenate([ztab.T, zdiff], axis=0)
    p = np.arange(TX)

    def cas(a):
        return np.cos(a) + np.sin(a)

    w = 2 * np.pi / TX
    har = cas(w * (p[:, None] * p[None, :] % TX)) / math.sqrt(TX)
    wmain = np.zeros((2, TX, GX, 2, SLOT))
    for X in range(GX):
        for t in range(NX + 1):
            for b in range(2):
                wmain[b, :, X, b, t] = har[:, (NX * X + t) % TX]
    wmain = wmain.reshape(2 * TX, GX * BLK)
    X = np.arange(GX)
    t12 = np.concatenate(
        [cas(w * p[:, None] * NX * X[None, :]), cas(-w * p[:, None] * NX * X[None, :])], axis=0
    ) / math.sqrt(TX)
    lane = np.arange(NY)
    cosx = np.where(lane[None, :] < NX, np.cos(w * p[:, None] * lane[None, :]), 0.0)
    sinx = np.where(lane[None, :] < NX, np.sin(w * p[:, None] * lane[None, :]), 0.0)
    cs = np.concatenate([cosx, sinx], axis=0)
    lam = (
        (2 - 2 * np.cos(np.pi * m[:, None] / NZ)) + (2 - 2 * np.cos(w * p[None, :]))
    ) * ASPECT
    zero = lam <= 0
    lam = np.where(zero, 0.5, lam)
    lnr = -2.0 * np.arcsinh(np.sqrt(lam) / 2.0)
    coef = np.where(zero, 0.0, -1.0 / (2.0 * np.sinh(-lnr)))
    lnr = lnr.reshape(2, GX, TX).transpose(1, 0, 2).reshape(GX, 2 * TX)
    coef = coef.reshape(2, GX, TX).transpose(1, 0, 2).reshape(GX, 2 * TX)
    misc = np.zeros((GX, 2 * TX, NY))
    for k in range(8):
        misc[:, :, k] = np.exp(lnr * (1 << k))
    misc[:, :, 8] = coef
    rowtab = np.zeros((GX, 8, 2 * TX))
    rowtab[:, 0] = NY * lnr
    rowtab[:, 1] = 1.0 / (1.0 - np.exp(lnr * TY))
    misc[:, :, 9] = lnr
    own = np.concatenate([misc, rowtab[:, :, :NY], rowtab[:, :, NY:]], axis=1)

    def f(a):
        return jnp.asarray(np.asarray(a, np.float32))

    return dict(
        ztab=f(ztab),
        zback=f(zback),
        wmain=f(wmain),
        wback=f(wmain.T),
        t12=f(t12),
        t12t=f(t12.T),
        cs=f(cs),
        own=f(own),
    )


def iota(shape, dim):
    return lax.broadcasted_iota(jnp.int32, shape, dim)


def dot(a, b):
    return jnp.dot(a, b, precision=HIGHEST, preferred_element_type=F32)


def field_row(fields, f, x):
    return fields[pl.ds(f * ROWS + x, NZ, stride=NX), :]


def pair_of(f0, lo, hi):
    d1, d2, d3 = (h - l for l, h in zip(lo, hi))
    s1, s2, s3 = (h + l for l, h in zip(lo, hi))
    return (45.0 * d1 - 9.0 * d2 + d3, 20.0 * f0 - 15.0 * s1 + 6.0 * s2 - s3)


def star_row(x, rows, ylo, yhi, slot, velocity, zs, lane):
    f0 = rows[x + 3]
    zs[8 : 8 + NZ, :] = f0
    zs[0:8, :] = jnp.broadcast_to(f0[0:1], (8, NY))
    zs[8 + NZ : 16 + NZ, :] = jnp.broadcast_to(f0[NZ - 1 : NZ], (8, NY))
    au, bu, av, bv, aw, bw = velocity
    a, b = pair_of(
        f0, [rows[x + 3 - k] for k in (1, 2, 3)], [rows[x + 3 + k] for k in (1, 2, 3)]
    )
    total = au * a + bu * b
    where_lo = 16 * x + 3 * slot
    halo = jnp.where(
        lane >= 64,
        pltpu.roll(ylo, (125 - where_lo) % NY, 1),
        pltpu.roll(yhi, (NY - where_lo) % NY, 1),
    )
    lo = [pltpu.roll(jnp.where(lane >= NY - k, halo, f0), k, 1) for k in (1, 2, 3)]
    hi = [pltpu.roll(jnp.where(lane < k, halo, f0), NY - k, 1) for k in (1, 2, 3)]
    a, b = pair_of(f0, lo, hi)
    total = total + (av * a + bv * b)
    a, b = pair_of(
        f0,
        [zs[8 - k : 8 - k + NZ, :] for k in (1, 2, 3)],
        [zs[8 + k : 8 + k + NZ, :] for k in (1, 2, 3)],
    )
    return f0 - (total + (aw * a + bw * b))


def velocity_rows(fields, x):
    out = []
    for f in range(3):
        a = field_row(fields, f, x) * (DT / 60.0)
        out += [a, jnp.abs(a)]
    return out


def sides_kernel(u, v, w, h, q, xlo, xhi, ylo, yhi, fields, done, sems):
    done[...] = jnp.zeros_like(done)
    copies = [
        pltpu.make_async_copy(ref, fields.at[pl.ds(f * ROWS, ROWS)], sems.at[f])
        for f, ref in enumerate((u, v, w, h, q))
    ]
    for copy in copies:
        copy.start()
    for copy in copies:
        copy.wait()
    for f in range(5):
        for i in range(3):
            n = f * 3 + i
            xlo[n * NZ : (n + 1) * NZ, :] = field_row(fields, f, 5 + i)
            xhi[n * NZ : (n + 1) * NZ, :] = field_row(fields, f, i)
    lane = iota((NZ, NY), 1)
    tlo = jnp.zeros((NZ, NY), F32)
    thi = jnp.zeros((NZ, NY), F32)
    for x in range(NX):
        for f in range(5):
            at = 16 * x + 3 * f
            row = field_row(fields, f, x)
            mask = (lane >= at) & (lane < at + 3)
            tlo = jnp.where(mask, pltpu.roll(row, (at - 125) % NY, 1), tlo)
            thi = jnp.where(mask, pltpu.roll(row, at, 1), thi)
    ylo[0:NZ, :] = tlo
    yhi[0:NZ, :] = thi


def pack_kernel(
    drops_in, cells, counts, own, after, up, down, mid, part, tabs, drops, sems
):
    copies = [
        pltpu.make_async_copy(drops_in, drops, sems.at[0]),
        pltpu.make_async_copy(own.at[lax.axis_index("gx")], tabs, sems.at[1]),
    ]
    for copy in copies:
        copy.start()
    copies[0].wait()
    for out, at, r, s in (
        [(up, r * SLOT, r, 2) for r in range(3)]
        + [(down, r * SLOT, r, 0) for r in range(3)]
        + [(mid, 0, 1, 1), (part, 0, 2, 1), (part, 16, 0, 1)]
    ):
        for a in range(10):
            out[at + a : at + a + 1, :] = drops[r, a, s : s + 1, :]
        out[at + 10 : at + 11, :] = cells[r, s : s + 1, :].astype(F32)
        out[at + 11 : at + 12, :] = jnp.full((1, CAP), counts[r, s], jnp.int32).astype(F32)
    for out, at, rows in ((up, 36, 4), (down, 36, 4), (mid, 12, 4), (part, 12, 4), (part, 28, 4)):
        out[at : at + rows, :] = jnp.zeros((rows, CAP), F32)
    copies[1].wait()


def hop_kernel(up, down, after, up_out, down_out, done):
    done[...] = jnp.zeros_like(done)


def block_of(msg, n):
    return (
        msg[n * SLOT : n * SLOT + 10, :],
        msg[n * SLOT + 10 : n * SLOT + 11, :],
        msg[n * SLOT + 11 : n * SLOT + 12, :],
    )


def relay_kernel(part, mlo, mhi, after, up, down, done):
    done[...] = jnp.zeros_like(done)
    for n, (out, r) in enumerate(((up, 2), (down, 0))):
        out[0:12, :] = mlo[r * SLOT : (r + 1) * SLOT, :]
        out[12:24, :] = mhi[r * SLOT : (r + 1) * SLOT, :]
        out[24:40, :] = part[n * 16 : (n + 1) * 16, :]


def wind_kernel(fields, xlo, xhi, ylo_in, yhi_in, ztab, east_s, north_s, rise_s, send, done, zs):
    done[...] = jnp.zeros_like(done)
    lane = iota((NZ, NY), 1)
    level = iota((NZ, NY), 0)
    ylo = ylo_in[0:NZ, :]
    yhi = yhi_in[0:NZ, :]
    vel = [velocity_rows(fields, x) for x in range(NX)]
    for f in range(3):
        rows = [xlo[(f * 3 + i) * NZ : (f * 3 + i + 1) * NZ, :] for i in range(3)]
        rows += [field_row(fields, f, x) for x in range(NX)]
        rows += [xhi[(f * 3 + i) * NZ : (f * 3 + i + 1) * NZ, :] for i in range(3)]
        for x in range(NX):
            star = star_row(x, rows, ylo, yhi, f, vel[x], zs.at[f * NX + x], lane)
            if f == 2:
                star = jnp.where(level == NZ - 1, 0.0, star)
            (east_s, north_s, rise_s)[f][pl.ds(x, NZ, stride=NX), :] = star
    tiles = []
    ext = jnp.zeros((NZ, NY), F32)
    for x in range(NX):
        east = field_row(east_s, 0, x)
        north = field_row(north_s, 0, x)
        rise = field_row(rise_s, 0, x)
        d = east + north + rise
        if x > 0:
            d = d - field_row(east_s, 0, x - 1)
        d = d - jnp.where(lane == 0, 0.0, pltpu.roll(north, 1, 1))
        d = d - jnp.where(level == 0, 0.0, pltpu.roll(rise, 1, 0))
        tiles.append(d)
        ext = jnp.where(lane == x, -pltpu.roll(north, (x + 1) % NY, 1), ext)
    tiles.append(-field_row(east_s, 0, NX - 1))
    tiles.append(ext)
    hat = dot(ztab[...], jnp.concatenate(tiles, axis=1))
    zeros = jnp.zeros((GX, NY), F32)
    for b in range(2):
        for t in range(SLOT):
            if t < NX + 2:
                val = hat[b * GX : (b + 1) * GX, t * NY : (t + 1) * NY]
            else:
                val = zeros
            send[pl.ds(b * SLOT + t, GX, stride=BLK), :] = val


def own_tables(tabs):
    n = 2 * TX
    return tabs.at[0:n], tabs.at[n : n + 16]


def scan_kernel(recv, wmain, t12, cs, tabs, after, msg, keep, kink, done):
    done[...] = jnp.zeros_like(done)
    misc, rowtab = own_tables(tabs)
    lane = iota((2 * TX, NY), 1)
    d = dot(wmain[...], recv[...])
    ends = []
    for b in range(2):
        e16 = recv[pl.ds(b * SLOT + NX + 1, GX, stride=BLK), :]
        prod = dot(t12[...], e16) * cs[...]
        ends.append(jnp.sum(prod[:TX] + prod[TX:], axis=1, keepdims=True))
    e = jnp.concatenate(ends, axis=0)
    fwd = d
    bwd = d
    for k in range(7):
        s = 1 << k
        a = jnp.broadcast_to(misc[:, k : k + 1], (2 * TX, NY))
        fwd = fwd + jnp.where(lane >= s, a * pltpu.roll(fwd, s, 1), 0.0)
        bwd = bwd + jnp.where(lane < NY - s, a * pltpu.roll(bwd, NY - s, 1), 0.0)
    r1 = misc[:, 0:1]
    r128 = misc[:, 7:8]
    out_right = r1 * fwd[:, NY - 1 : NY] + e
    out_left = bwd[:, 0:1] + r128 * e
    from_end = float(NY) - lane.astype(F32)
    keep[...] = fwd + bwd - d + jnp.exp(from_end * misc[:, 9:10]) * e
    lane1 = lane[:TX]
    table = jnp.zeros((TX, NY), F32)
    for b in range(2):
        table = jnp.where(lane1 == b, out_right[b * TX : (b + 1) * TX], table)
        table = jnp.where(lane1 == 2 + b, out_left[b * TX : (b + 1) * TX], table)
    d8 = d[0:8]
    e8 = e[0:8]
    lane8 = iota((8, NY), 1)
    lanef = lane8.astype(F32)
    s0 = jnp.sum(d8, axis=1, keepdims=True) + e8
    s1 = jnp.sum(d8 * lanef, axis=1, keepdims=True) + float(NY) * e8
    top = jnp.where(lane8 == 4, s0, jnp.where(lane8 == 5, s1, table[0:8]))
    table = jnp.concatenate([top, table[8:]], axis=0)
    turned = table.T[0:8]
    for y in range(GY):
        msg[y * 8 : (y + 1) * 8, :] = turned
    apart = jnp.abs(iota((NY, NY), 0) - iota((NY, NY), 1)).astype(F32)
    kink[...] = dot(d8, apart) + e8 * (float(NY) - lanef)


def solve_kernel(got, keep, kink, wback, t12t, cs, tabs, after, send, done):
    done[...] = jnp.zeros_like(done)
    misc, rowtab = own_tables(tabs)
    here = lax.axis_index("gy")
    first = (lax.axis_index("gx") == 0).astype(F32)
    who = iota((GY, 2 * TX), 0)
    def rows(k):
        return jnp.concatenate([got[y * 8 + k : y * 8 + k + 1, :] for y in range(GY)], axis=0)

    all_right = jnp.concatenate([rows(0), rows(1)], axis=1)
    all_left = jnp.concatenate([rows(2), rows(3)], axis=1)
    s0 = rows(4)[:, 0:1]
    s1 = rows(5)[:, 0:1]
    lnr = jnp.concatenate([rowtab[0:1, :], rowtab[8:9, :]], axis=1)
    inv = jnp.concatenate([rowtab[1:2, :], rowtab[9:10, :]], axis=1)
    after = ((here - who - 1) & (GY - 1)).astype(F32)
    before = ((who - here - 1) & (GY - 1)).astype(F32)
    in_left = jnp.sum(jnp.exp(after * lnr) * all_right, axis=0, keepdims=True) * inv
    in_right = jnp.sum(jnp.exp(before * lnr) * all_left, axis=0, keepdims=True) * inv
    own_right = jnp.sum(jnp.where(who == here, all_right, 0.0), axis=0, keepdims=True)
    row = iota((8, 2 * TX), 0)
    turned = jnp.where(row == 0, in_left, jnp.where(row == 1, in_right, own_right)).T
    in_left = turned[:, 0:1]
    in_right = turned[:, 1:2]
    coef = misc[:, 8:9]
    lnc = jnp.broadcast_to(misc[:, 9:10], (2 * TX, NY))
    at = iota((2 * TX, NY), 1).astype(F32)
    pres = coef * (
        keep[...] + jnp.exp(at * lnc) * in_left + jnp.exp((float(NY) - at) * lnc) * in_right
    )
    edge = coef * (turned[:, 2:3] + misc[:, 7:8] * in_left + in_right)
    who1 = iota((GY, 1), 0)
    far = (NY * ((here - who1) & (GY - 1))).astype(F32)
    mine = who1 == here
    sum0 = jnp.sum(s0, axis=0, keepdims=True)
    own0 = jnp.sum(jnp.where(mine, s0, 0.0), axis=0, keepdims=True)
    own1 = jnp.sum(jnp.where(mine, s1, 0.0), axis=0, keepdims=True)
    lin = 0.5 * (sum0 - own0) + jnp.sum(s1 - far * s0, axis=0, keepdims=True) * (1.0 / TY)
    quad = sum0 * (0.5 / TY)
    lanef = iota((8, NY), 1).astype(F32)
    top = 0.5 * kink[...] + lanef * (lin - lanef * quad)
    edge0 = 0.5 * (float(NY) * own0 - own1) + float(NY) * (lin - float(NY) * quad)
    row8 = iota((8, NY), 0)
    top = pres[0:8] + jnp.where(row8 == 0, first * top, 0.0)
    pres = jnp.concatenate([top, pres[8:]], axis=0)
    row1 = iota((2 * TX, 1), 0)
    edge = edge + jnp.where(row1 == 0, first * edge0, 0.0)
    send[...] = dot(wback[...], pres)
    for b in range(2):
        eb = edge[b * TX : (b + 1) * TX]
        spread = jnp.concatenate([cs[0:TX, :] * eb, cs[TX:, :] * eb], axis=0)
        send[pl.ds(b * SLOT + NX + 1, GX, stride=BLK), :] = dot(t12t[...], spread)


def store_table(lhs, n, table):
    turned = table.T
    hi = turned.astype(BF16)
    lhs[2 * n * NY : (2 * n + 1) * NY, :] = hi
    lhs[(2 * n + 1) * NY : (2 * n + 2) * NY, :] = (turned - hi.astype(F32)).astype(BF16)


def masks_of(cells):
    width = cells.shape[1]
    rowid = ((cells >> 7) & (NX - 1)) * NZ + (cells >> 10)
    each = iota((ROWS, width), 0).astype(F32).astype(BF16)
    hot = jnp.where(
        each == rowid.astype(F32).astype(BF16), jnp.array(1.0, BF16), jnp.array(0.0, BF16)
    )
    pick = iota((NY, width), 0) == (cells & (NY - 1))
    return hot, pick


def gather_all(lhs, count, cell, air):
    for n in range(9):
        for at in range(0, CAP, CHUNK):
            hot, pick = masks_of(cell[n : n + 1, at : at + CHUNK])
            got = jnp.dot(lhs[...], hot, preferred_element_type=F32)
            for f in range(count):
                a = 2 * f * NY
                both = got[a : a + NY] + got[a + NY : a + 2 * NY]
                air[f, n : n + 1, at : at + CHUNK] = jnp.sum(
                    jnp.where(pick, both, 0.0), axis=0, keepdims=True
                )


CHUNK = 512


def heat_kernel(fields, ylo_in, yhi_in, xlo, xhi, after, stars, lhs, done, zs):
    done[...] = jnp.zeros_like(done)
    lane = iota((NZ, NY), 1)
    ylo = ylo_in[0:NZ, :]
    yhi = yhi_in[0:NZ, :]
    vel = [velocity_rows(fields, x) for x in range(NX)]

    for f in range(2):
        rows = [xlo[(f * 3 + i + 9) * NZ : (f * 3 + i + 10) * NZ, :] for i in range(3)]
        rows += [field_row(fields, 3 + f, x) for x in range(NX)]
        rows += [xhi[(f * 3 + i + 9) * NZ : (f * 3 + i + 10) * NZ, :] for i in range(3)]
        for x in range(NX):
            star = star_row(x, rows, ylo, yhi, 3 + f, vel[x], zs.at[f * NX + x], lane)
            at = (f * NX + x) * NZ
            stars[at : at + NZ, :] = star
        store_table(lhs, f, stars[f * ROWS : (f + 1) * ROWS, :])


def unpack_kernel(mid, mlo, mhi, clo, chi, after, cell_out, state):
    for r in range(3):
        for s in range(3):
            n = r * 3 + s
            if r == 1:
                block = block_of((mlo, mid, mhi)[s], (1, 0, 1)[s])
            else:
                block = block_of((clo, None, chi)[r], (0, 2, 1)[s])
            values, cell, count = block
            for a in range(10):
                state[a, n : n + 1, :] = values[a : a + 1]
            cell_out[n : n + 1, :] = cell.astype(jnp.int32)
            slot = iota((1, CAP), 1).astype(F32)
            state[10, n : n + 1, :] = jnp.where(slot < count, 1.0, 0.0)


def growth_kernel(lhs, cell, state, state_out, gain, air):
    gather_all(lhs, 2, cell, air)
    live = state[10]
    radius = state[6]
    cubed = radius * radius * radius
    keeping = jnp.exp(-DT / (RELAX_TIME * radius * radius))
    saturation = air[1] * jnp.exp(-SATURATION_RATE * air[0]) - 1.0
    squared = radius * radius + GROWTH * (
        saturation - CURVATURE / radius + SOLUTE_EFFECT * state[8] / cubed
    )
    new_radius = jnp.sqrt(jnp.maximum(squared, RADIUS_FLOOR * RADIUS_FLOOR))
    gain[...] = live * state[7] * (new_radius * new_radius * new_radius - cubed)
    state_out[6] = new_radius * live
    state_out[7] = state[7] * live
    state_out[8] = state[8] * live
    state_out[9] = (state[9] + DT) * live
    for a in range(3):
        state_out[a] = state[a] * live
        state_out[3 + a] = state[3 + a] * (keeping * live)
    state_out[10] = (1.0 - keeping) * live


def scatter_kernel(stars, cell, gain, heat_next, moist_next, acc):
    acc[...] = jnp.zeros_like(acc)

    for n in range(9):
        for at in range(0, CAP, CHUNK):
            hot, pick = masks_of(cell[n : n + 1, at : at + CHUNK])
            g = gain[n : n + 1, at : at + CHUNK]
            hi = g.astype(BF16).astype(F32)
            z = jnp.concatenate(
                [
                    jnp.where(pick, hi, 0.0).astype(BF16),
                    jnp.where(pick, g - hi, 0.0).astype(BF16),
                ],
                axis=0,
            )
            acc[...] += lax.dot_general(
                hot, z, (((1,), (1,)), ((), ())), preferred_element_type=F32
            )
    for x in range(NX):
        a = x * NZ
        condensed = acc[a : a + NZ, 0:NY] + acc[a : a + NZ, NY:]
        heat_next[pl.ds(x, NZ, stride=NX), :] = stars[a : a + NZ, :] + HEAT_LOAD * condensed
        moist_next[pl.ds(x, NZ, stride=NX), :] = (
            stars[ROWS + a : ROWS + a + NZ, :] - MOIST_LOAD * condensed
        )


def final_kernel(
    recv, east_s, north_s, rise_s, zback, cell, state, east_next, north_next, up_next, drops_out, lhs, next_rows, air
):
    lane = iota((NZ, NY), 1)
    tiles = []
    for t in range(NX + 2):
        tiles.append(
            jnp.concatenate(
                [recv[pl.ds(b * SLOT + t, GX, stride=BLK), :] for b in range(2)], axis=0
            )
        )
    both = dot(zback[...], jnp.concatenate(tiles, axis=1))
    pres = [both[:NZ, t * NY : (t + 1) * NY] for t in range(NX + 2)]
    edge = pres[NX + 1]
    for x in range(NX):
        east = field_row(east_s, 0, x) - (pres[x + 1] - pres[x]) * ASPECT
        ahead = pltpu.roll(
            jnp.where(lane == 0, pltpu.roll(edge, (NY - x) % NY, 1), pres[x]), NY - 1, 1
        )
        north = field_row(north_s, 0, x) - (ahead - pres[x])
        rise = field_row(rise_s, 0, x) - both[NZ:, x * NY : (x + 1) * NY]
        for f, (val, ref) in enumerate(
            ((east, east_next), (north, north_next), (rise, up_next))
        ):
            ref[pl.ds(x, NZ, stride=NX), :] = val
            next_rows[f, x * NZ : (x + 1) * NZ, :] = val
    for f in range(3):
        store_table(lhs, f, next_rows[f])

    gather_all(lhs, 3, cell, air)
    mix = state[10]
    for a in range(3):
        speed = air[a] * mix + state[3 + a]
        offset = state[a] + DT * speed
        for r in range(3):
            drops_out[r, 3 + a] = speed[3 * r : 3 * r + 3]
            drops_out[r, a] = offset[3 * r : 3 * r + 3]
    for a in range(6, 10):
        for r in range(3):
            drops_out[r, a] = state[a, 3 * r : 3 * r + 3, :]


VM = pl.BlockSpec(memory_space=pltpu.VMEM)
SM = pl.BlockSpec(memory_space=pltpu.SMEM)
ANY = pl.BlockSpec(memory_space=pl.ANY)
HBM = pl.BlockSpec(memory_space=pltpu.HBM)


def sds(*shape, dtype=F32):
    return jax.ShapeDtypeStruct(shape, dtype)


TOKEN = sds(8, NY)


def call(kernel, name, us, out_shape, in_specs, scratch=(), mib=6, aliases=None, outs=None):
    return pl.pallas_call(
        kernel,
        out_shape=out_shape,
        in_specs=in_specs,
        out_specs=tuple(outs or [VM] * len(out_shape)),
        scratch_shapes=list(scratch),
        input_output_aliases=aliases or {},
        compiler_params=pltpu.CompilerParams(vmem_limit_bytes=mib * 1024 * 1024),
        cost_estimate=pl.CostEstimate(
            flops=int(us * 5e8), bytes_accessed=int(us * 2e6), transcendentals=0
        ),
        name=name,
    )


def ring(axis, shift):
    count = lax.axis_size(axis)
    return [(i, (i + shift) % count) for i in range(count)]


def per_device(u, v, w, h, q, droplets, cells, counts):
    tab = make_tables()
    u, v, w, h, q = (a.reshape(ROWS, NY) for a in (u, v, w, h, q))
    drops = droplets.transpose(0, 2, 1, 3)
    xlo, xhi, ylo, yhi, fields, done = call(
        sides_kernel,
        "sides",
        2.0,
        (
            sds(15 * NZ, NY), sds(15 * NZ, NY), sds(1 * NZ, NY), sds(1 * NZ, NY),
            sds(5 * ROWS, NY), TOKEN,
        ),
        [HBM] * 5,
        [pltpu.SemaphoreType.DMA((5,))],
        60,
    )(u, v, w, h, q)
    xlo = lax.ppermute(xlo, "gx", ring("gx", 1))
    xhi = lax.ppermute(xhi, "gx", ring("gx", -1))
    ylo = lax.ppermute(ylo, "gy", ring("gy", 1))
    yhi = lax.ppermute(yhi, "gy", ring("gy", -1))
    up, down, mid, part, tabs = call(
        pack_kernel,
        "pack",
        2.5,
        (sds(40, CAP), sds(40, CAP), sds(16, CAP), sds(32, CAP), sds(2 * TX + 16, NY)),
        [HBM, VM, SM, HBM, ANY],
        [pltpu.VMEM((3, 10, 3, CAP), F32), pltpu.SemaphoreType.DMA((2,))],
        60,
    )(drops, cells, counts, tab["own"], done)
    east_s, north_s, rise_s, send, done = call(
        wind_kernel,
        "winds",
        3.0,
        (sds(ROWS, NY), sds(ROWS, NY), sds(ROWS, NY), sds(GX * BLK, NY), TOKEN),
        [VM] * 6,
        [pltpu.VMEM((3 * NX, NZ + 16, NY), F32)],
    )(fields, xlo, xhi, ylo, yhi, tab["ztab"])
    recv = lax.all_to_all(send.reshape(GX, BLK, NY), "gx", 0, 0, tiled=True)
    up, down, done = call(
        hop_kernel,
        "hop",
        0.5,
        (sds(40, CAP), sds(40, CAP), TOKEN),
        [ANY] * 3,
        aliases={0: 0, 1: 1},
        outs=[ANY, ANY, VM],
    )(up, down, done)
    mlo = lax.ppermute(up, "gy", ring("gy", 1))
    mhi = lax.ppermute(down, "gy", ring("gy", -1))
    msg, keep, kink, done = call(
        scan_kernel,
        "scan",
        2.0,
        (sds(8 * GY, NY), sds(2 * TX, NY), sds(8, NY), TOKEN),
        [VM] * 5 + [ANY],
    )(
        recv.reshape(GX * BLK, NY), tab["wmain"], tab["t12"], tab["cs"], tabs, done
    )
    got = lax.all_to_all(msg.reshape(GY, 8, NY), "gy", 0, 0, tiled=True)
    stars_hq, lhs, done = call(
        heat_kernel,
        "heat",
        4.0,
        (sds(2 * ROWS, NY), sds(4 * NY, ROWS, dtype=BF16), TOKEN),
        [VM] * 5 + [ANY],
        [pltpu.VMEM((2 * NX, NZ + 16, NY), F32)],
    )(fields, ylo, yhi, xlo, xhi, done)
    cup, cdown, done = call(
        relay_kernel, "relay", 1.0, (sds(40, CAP), sds(40, CAP), TOKEN), [VM] * 3 + [ANY]
    )(part, mlo, mhi, done)
    clo = lax.ppermute(cup, "gx", ring("gx", 1))
    chi = lax.ppermute(cdown, "gx", ring("gx", -1))
    send, done = call(
        solve_kernel, "solve", 2.0, (sds(GX * BLK, NY), TOKEN), [VM] * 7 + [ANY]
    )(
        got.reshape(8 * GY, NY), keep, kink, tab["wback"], tab["t12t"], tab["cs"], tabs,
        done,
    )
    recv = lax.all_to_all(send.reshape(GX, BLK, NY), "gx", 0, 0, tiled=True)
    cell_in, state = call(
        unpack_kernel,
        "unpack",
        1.0,
        (sds(9, CAP, dtype=jnp.int32), sds(11, 9, CAP)),
        [VM] * 5 + [ANY],
    )(mid, mlo, mhi, clo, chi, done)
    state, gain = call(
        growth_kernel,
        "growth",
        5.0,
        (sds(11, 9, CAP), sds(9, CAP)),
        [VM] * 3,
        [pltpu.VMEM((2, 9, CAP), F32)],
    )(lhs, cell_in, state)
    heat_next, moist_next = call(
        scatter_kernel,
        "scatter",
        4.0,
        (sds(ROWS, NY), sds(ROWS, NY)),
        [VM] * 3,
        [pltpu.VMEM((ROWS, 2 * NY), F32)],
    )(stars_hq, cell_in, gain)
    east_next, north_next, up_next, drops_out = call(
        final_kernel,
        "final",
        8.0,
        (sds(ROWS, NY), sds(ROWS, NY), sds(ROWS, NY), sds(3, 10, 3, CAP)),
        [VM] * 7,
        [
            pltpu.VMEM((6 * NY, ROWS), BF16),
            pltpu.VMEM((3, ROWS, NY), F32),
            pltpu.VMEM((3, 9, CAP), F32),
        ],
        aliases={1: 0, 2: 1, 3: 2},
    )(recv.reshape(GX * BLK, NY), east_s, north_s, rise_s, tab["zback"], cell_in, state)
    out = (
        a.reshape(NZ, NX, NY) for a in (east_next, north_next, up_next, heat_next, moist_next)
    )
    return (*out, drops_out.transpose(0, 2, 1, 3))


def solution(mesh):
    grid = P(None, "gx", "gy")
    blocks = P("gx", "gy", None, None)
    return jax.shard_map(
        per_device,
        mesh=mesh,
        in_specs=(grid,) * 5 + (blocks, P("gx", "gy", None), P("gx", "gy")),
        out_specs=(grid,) * 5 + (blocks,),
        check_vma=False,
    )
```
